768 devices in a mesh: dp: 64 (over x, y, z_hi), enc: 12 (over z_lo, core).
Axes of the slice: x: 4, y: 8, z: 12 (z_hi: 2, z_lo: 6; z = z_hi * 6 + z_lo), core: 2. Of those that a mesh axis runs over, the one named last changes fastest.
Arguments:
- patches: bfloat16 [3072, 196, 768], P(('dp', 'enc')), may hold values from -6 to 6
- item_counts: int32 [768], P(('dp', 'enc')), may hold values from 1 to 4, as said below
- item_ids: int32 [3072], P(('dp', 'enc')), may hold values from 0 to 65535
- block_dest: int32 [12288], P(('dp', 'enc')), may hold values from 0 to 11, as said below
- enc_weight: bfloat16 [12, 768, 768], P('enc'), may hold values from -0.21875 to 0.21875
- enc_bias: float32 [12, 768], P('enc'), may hold values from -3 to 3
- enc_gain: float32 [12, 768], P('enc'), may hold values from 0.5 to 1.5
- item_bias: float32 [65536], replicated, may hold values from -2 to 2
- user_state: bfloat16 [196608, 768], P(('dp', 'enc')), may hold values from -6 to 6
- user_proj: bfloat16 [768, 768], replicated, may hold values from -0.21875 to 0.21875
- positives: int32 [196608], P(('dp', 'enc')), may hold values from 0 to 999
Outputs:
- d_user_state: bfloat16 [196608, 768], P(('dp', 'enc'))
- grad_weight: float32 [12, 768, 768], P('enc', 'dp')
- grad_bias: float32 [12, 768], P('enc')
- grad_gain: float32 [12, 768], P('enc')
The draws below stay inside these ranges and needn't reach their ends.
Inputs may be any that keep to these rules, and one draw needn't show every extreme that they name: `item_counts`: live items of each device; device 0 holds 4. `block_dest`: among the blocks of one device at most 2 name the same expert; in every group of devices along enc some expert receives 2 live blocks from every device of the group.
All inputs are finite; a program needn't handle non-finite values.
Results may differ from the reference program's by a relative error of at most 0.017.
Values may be sent and summed in bfloat16 or wider, within the bound.
A program may use at most 32 MiB of HBM per device.

```python
import math
import jax
import jax.numpy as jnp
import numpy as np
from jax import lax

D = 768
PATCH_IN = 768
PATCHES = 196
BLOCK_ROWS = 49
BLOCKS_ITEM = 4
ITEMS_DEV = 4
BLOCKS_DEV = 16
CAP = 2
ENCODERS = 12
ITEMS = 3072
USERS_DEV = 256
USERS = 196608
VOCAB = 65536
N_DP = 64
N_ENC = 12


def draw_item_counts(key, part):
    key = jax.random.fold_in(key, 11)
    counts = jax.random.randint(key, (N_DP * N_ENC,), 1, ITEMS_DEV + 1)
    return counts.at[0].set(ITEMS_DEV).astype(jnp.int32)


def draw_block_dest(key, part):
    key = jax.random.fold_in(key, 23)
    hot_key, perm_key, first_key = jax.random.split(key, 3)
    hottest = jax.random.randint(hot_key, (N_DP,), 0, N_ENC)
    hot_device = jnp.repeat(hottest, N_ENC)
    slot_owner = jnp.arange((N_ENC - 1) * CAP, dtype=jnp.int32) // CAP

    def device_row(hot_one, perm_one, first_one):
        other_slots = slot_owner + (slot_owner >= hot_one).astype(jnp.int32)
        other_slots = jax.random.permutation(perm_one, other_slots)
        slot_row = jnp.concatenate([jnp.full((CAP,), hot_one, jnp.int32), other_slots[:BLOCKS_DEV - CAP]])
        first_item = jax.random.permutation(first_one, slot_row[:BLOCKS_ITEM])
        return jnp.concatenate([first_item, slot_row[BLOCKS_ITEM:]])
    devices = N_DP * N_ENC
    rows_all = jax.vmap(device_row)(hot_device, jax.random.split(perm_key, devices), jax.random.split(first_key, devices))
    return rows_all.reshape(-1).astype(jnp.int32)


def touch_ends(entries, stream_key, low, top_value):
    longest = entries.shape.index(max(entries.shape))
    spots = []
    for shift in (0, 1):
        where = [jax.random.randint(jax.random.fold_in(stream_key, axis), (), 0, length) for axis, length in enumerate(entries.shape)]
        where[longest] = (where[longest] + shift) % entries.shape[longest]
        spots.append(tuple(where))
    return entries.at[spots[0]].set(low).at[spots[1]].set(top_value)


def levels(key, shape, cuts, smallest, high):
    def one(axis_at, parts):
        heights = jax.random.uniform(jax.random.fold_in(jax.random.fold_in(key, 6), axis_at), (parts,), jnp.float32, smallest / len(cuts), high / len(cuts))
        return jnp.repeat(jnp.exp(heights), shape[axis_at] // parts).reshape((-1,) + (1,) * (len(shape) - axis_at - 1))

    factor_of = one(*cuts[0])
    for cut in cuts[1:]:
        factor_of = factor_of * one(*cut)
    return factor_of


def cumulative_ranks(number_of, slope):
    loads = [(1 << 20) // math.isqrt(standing ** slope) + 1 for standing in range(1, number_of + 1)]
    scale = 1 + sum(loads) // (1 << 30)
    return np.cumsum(np.array([max(1, weight // scale) for weight in loads]))


def ranked(own_key, extent, number_of, lean):
    listing = cumulative_ranks(number_of, lean)
    pick = jax.random.randint(jax.random.fold_in(own_key, 1), extent, 0, int(listing[number_of - 1]))
    standing = jnp.searchsorted(jnp.asarray(listing, jnp.int32), pick, side="right")
    return jax.random.permutation(jax.random.fold_in(own_key, 2), number_of)[standing].astype(jnp.int32)


def normal_values(own_key, shape, scale, limit, cuts=(), kind=jnp.bfloat16):
    entries = jax.random.normal(own_key, shape, jnp.float32) * scale
    if len(cuts) > 0:
        entries = levels(own_key, shape, cuts, -0.22, 0.18) * entries
    return jnp.clip(entries, min=-limit, max=limit).astype(kind)


def setup_inputs(seed: int = 0) -> dict:
    key_list = jax.random.split(jax.random.key(seed), 12)
    return {
        "patches": normal_values(key_list[0], (ITEMS, PATCHES, PATCH_IN), 1.0, 6.0, ((0, 768),)),
        "item_counts": draw_item_counts(jax.random.fold_in(key_list[11], 71), 0),
        "item_ids": touch_ends(ranked(key_list[2], (ITEMS,), VOCAB, 2), jax.random.fold_in(key_list[2], 3), 0, VOCAB - 1).astype(jnp.int32),
        "block_dest": draw_block_dest(jax.random.fold_in(key_list[11], 71), 0),
        "enc_weight": normal_values(key_list[4], (ENCODERS, PATCH_IN, D), PATCH_IN ** -0.5, 0.21875, ((0, 12),)),
        "enc_bias": normal_values(key_list[5], (ENCODERS, D), 0.5, 3.0, ((0, 12),), jnp.float32),
        "enc_gain": jnp.clip(1.0 + 0.1 * jax.random.normal(key_list[6], (ENCODERS, D), jnp.float32), 0.5, 1.5),
        "item_bias": jnp.clip(jax.random.uniform(key_list[7], (VOCAB,), jnp.float32, -2.0, 2.0), -2.0, 2.0),
        "user_state": normal_values(key_list[8], (USERS, D), 1.0, 6.0, ((0, 768),)),
        "user_proj": normal_values(key_list[9], (D, D), D ** -0.5, 0.21875),
        "positives": touch_ends(jax.random.randint(key_list[10], (USERS,), 0, 1000), jax.random.fold_in(key_list[10], 1), 0, 999).astype(jnp.int32),
    }


score_scale = 0.1
loss_weight = 16.0
norm_eps = 1e-05

def pooled_rows(projected, bias_rows, gain_rows):
    shifted = projected + bias_rows
    center = lax.optimization_barrier(jnp.mean(shifted, axis=-1, keepdims=True))
    deviation = shifted - center
    variance = lax.optimization_barrier(jnp.mean(deviation * deviation, axis=-1, keepdims=True))
    normed = deviation * lax.rsqrt(variance + norm_eps) * gain_rows
    return lax.optimization_barrier(jnp.sum(jax.nn.gelu(normed, approximate=True), axis=-2))

def reference(patches, item_counts, item_ids, block_dest, enc_weight, enc_bias, enc_gain, item_bias, user_state, user_proj, positives):
    devices = N_DP * N_ENC
    blocks_dev = ITEMS_DEV * BLOCKS_ITEM
    blocks = patches.reshape(devices, blocks_dev, BLOCK_ROWS, PATCH_IN)
    dests = block_dest.reshape(devices, blocks_dev)
    id_rows = item_ids.reshape(devices, ITEMS_DEV)
    users = user_state.reshape(devices, USERS_DEV, D)
    chosen = positives.reshape(devices, USERS_DEV)

    def device_step(totals, inputs):
        block_rows, dest_row, live_items, id_row, user_rows, chosen_row = inputs
        weights = enc_weight[dest_row].astype(jnp.float32)
        projected = jnp.einsum('brp,bpd->brd', block_rows.astype(jnp.float32), weights)
        bias_rows = enc_bias[dest_row][:, None, :]
        gain_rows = enc_gain[dest_row][:, None, :]
        pooled_out, backward = jax.vjp(pooled_rows, projected, bias_rows, gain_rows)
        partial_value = pooled_out.astype(jnp.bfloat16)
        summed = lax.optimization_barrier(jnp.sum(partial_value.astype(jnp.float32).reshape(ITEMS_DEV, BLOCKS_ITEM, D), axis=1))
        embed = (summed / PATCHES).astype(jnp.bfloat16)
        user_vec = jnp.dot(user_rows, user_proj, preferred_element_type=jnp.float32).astype(jnp.bfloat16)
        scores = jnp.dot(user_vec, embed.T, preferred_element_type=jnp.float32) * score_scale + item_bias[id_row][None, :]
        item_index = jnp.arange(ITEMS_DEV, dtype=jnp.int32)
        live_item = item_index < live_items
        target = (item_index[None, :] == (chosen_row % live_items)[:, None]).astype(jnp.float32)
        d_score = jnp.where(live_item[None, :], loss_weight * (jax.nn.sigmoid(scores) - target), 0.0).astype(jnp.bfloat16)
        d_embed = (jnp.dot(d_score.T, user_vec, preferred_element_type=jnp.float32) * score_scale).astype(jnp.bfloat16)
        d_user_vec = (jnp.dot(d_score, embed, preferred_element_type=jnp.float32) * score_scale).astype(jnp.bfloat16)
        d_user = jnp.dot(d_user_vec, user_proj.T, preferred_element_type=jnp.float32).astype(jnp.bfloat16)
        live_block = jnp.arange(blocks_dev, dtype=jnp.int32) // BLOCKS_ITEM < live_items
        d_block = jnp.repeat(d_embed.astype(jnp.float32), BLOCKS_ITEM, axis=0) / PATCHES
        d_block = jnp.where(live_block[:, None], d_block, 0.0)
        d_proj, d_bias, d_gain = backward(d_block)
        d_proj_low = d_proj.astype(jnp.bfloat16)
        terms = jnp.einsum('brp,brd->bpd', block_rows.astype(jnp.float32), d_proj_low.astype(jnp.float32))
        grad_w, grad_b, grad_g = totals
        grad_w = grad_w.at[dest_row].add(terms)
        grad_b = grad_b.at[dest_row].add(d_bias[:, 0, :])
        grad_g = grad_g.at[dest_row].add(d_gain[:, 0, :])
        return ((grad_w, grad_b, grad_g), d_user)
    start = (jnp.zeros((ENCODERS, PATCH_IN, D), jnp.float32), jnp.zeros((ENCODERS, D), jnp.float32), jnp.zeros((ENCODERS, D), jnp.float32))
    totals, d_users = lax.scan(device_step, start, (blocks, dests, item_counts, id_rows, users, chosen))
    grad_w, grad_b, grad_g = totals
    return (d_users.reshape(USERS, D), grad_w / N_DP, grad_b / N_DP, grad_g / N_DP)
```

```python
import jax
import jax.numpy as jnp
from jax import lax
from jax.experimental import pallas as pl
from jax.experimental.pallas import tpu as pltpu
from jax.sharding import PartitionSpec as P

NX, NY, NZ = 4, 8, 2
ROWS_DEV = 12
FOLD = 1152

D = 768
PATCH_IN = 768
PATCHES = 196
BLOCK_ROWS = 49
BLOCKS_ITEM = 4
ITEMS_DEV = 4


score_scale = 0.1
loss_weight = 16.0
norm_eps = 1e-05


def pooled_rows(projected, bias_rows, gain_rows):
    shifted = projected + bias_rows
    center = jnp.mean(shifted, axis=-1, keepdims=True)
    deviation = shifted - center
    variance = jnp.mean(deviation * deviation, axis=-1, keepdims=True)
    normed = deviation * lax.rsqrt(variance + norm_eps) * gain_rows
    return jnp.sum(jax.nn.gelu(normed, approximate=True), axis=-2)


def fold(rows):
    tail = rows[8:12]
    return jnp.concatenate([rows[0:8], jnp.concatenate([tail[:, :384], tail[:, 384:]], axis=0)], axis=1)


def unfold(folded):
    tail = folded[:, 768:]
    return jnp.concatenate([folded[:, :768], jnp.concatenate([tail[0:4], tail[4:8]], axis=1)], axis=0)


def reduce_kernel(
    g_ref, v_ref, out_ref, vout_ref,
    sx, rx, sy, ry, accx, sz, rz, vx, vy, vz,
    sem_sx, sem_rx, sem_sy, sem_ry, sem_z, sem_vsx, sem_vrx, sem_vsy, sem_vry, sem_vz,
):
    dp = lax.axis_index("dp")
    x = dp // (NY * NZ)
    y = (dp // NZ) % NY
    z = dp % NZ

    def at(xx, yy, zz):
        return {"dp": (xx * NY + yy) * NZ + zz}

    barrier = pltpu.get_barrier_semaphore()
    for d in range(1, NX):
        pl.semaphore_signal(barrier, inc=1, device_id=at((x + d) % NX, y, z))
    for d in range(1, NY):
        pl.semaphore_signal(barrier, inc=1, device_id=at(x, (y + d) % NY, z))
    pl.semaphore_signal(barrier, inc=1, device_id=at(x, y, 1 - z))

    def pack(xx):
        @pl.loop(0, NY)
        def _(k):
            first = pl.multiple_of((xx * NY + k) * 24, 8)
            chunk = g_ref[pl.ds(first, 24), :]
            sx[xx, k] = jnp.concatenate([fold(chunk[0:12]), fold(chunk[12:24])], axis=0).astype(jnp.bfloat16)

    vx[x] = v_ref[...]
    started = []
    for d in range(1, NX):
        to = (x + d) % NX
        pack(to)
        if d == 1:
            pl.semaphore_wait(barrier, NX + NY - 1)
        started.append(pltpu.make_async_remote_copy(
            src_ref=sx.at[to], dst_ref=rx.at[d - 1], send_sem=sem_sx.at[d - 1], recv_sem=sem_rx.at[d - 1],
            device_id=at(to, y, z)))
        started.append(pltpu.make_async_remote_copy(
            src_ref=v_ref, dst_ref=vx.at[x], send_sem=sem_vsx.at[d - 1], recv_sem=sem_vrx.at[d - 1],
            device_id=at(to, y, z)))
        started[-2].start()
        started[-1].start()
    pack(x)
    for copy in started:
        copy.wait_recv()

    vsum = (vx[0] + vx[1]) + (vx[2] + vx[3])
    vy[y] = vsum

    def sum_x(k, carry):
        total = (sx[x, k].astype(jnp.float32) + rx[0, k].astype(jnp.float32)) + (
            rx[1, k].astype(jnp.float32) + rx[2, k].astype(jnp.float32))
        accx[k] = total
        sy[k] = total.astype(jnp.bfloat16)
        return carry
    lax.fori_loop(0, NY, sum_x, 0)
    second = []
    for d in range(1, NY):
        to = (y + d) % NY
        second.append(pltpu.make_async_remote_copy(
            src_ref=sy.at[to], dst_ref=ry.at[d - 1], send_sem=sem_sy.at[d - 1], recv_sem=sem_ry.at[d - 1],
            device_id=at(x, to, z)))
        second.append(pltpu.make_async_remote_copy(
            src_ref=vy.at[y], dst_ref=vy.at[y], send_sem=sem_vsy.at[d - 1], recv_sem=sem_vry.at[d - 1],
            device_id=at(x, to, z)))
        second[-2].start()
        second[-1].start()
    total = accx[y]
    for d in range(1, NY):
        second[2 * d - 2].wait_recv()
        total = total + ry[d - 1].astype(jnp.float32)
    for d in range(1, NY):
        second[2 * d - 1].wait_recv()
    vz[0] = ((vy[0] + vy[1]) + (vy[2] + vy[3])) + ((vy[4] + vy[5]) + (vy[6] + vy[7]))
    sz[0] = total[0:8]
    sz[1] = total[8:16]
    last = [
        pltpu.make_async_remote_copy(
            src_ref=sz.at[1 - z], dst_ref=rz, send_sem=sem_z.at[0], recv_sem=sem_z.at[1], device_id=at(x, y, 1 - z)),
        pltpu.make_async_remote_copy(
            src_ref=vz.at[0], dst_ref=vz.at[1], send_sem=sem_vz.at[0], recv_sem=sem_vz.at[1],
            device_id=at(x, y, 1 - z)),
    ]
    for copy in last:
        copy.start()
    for copy in last:
        copy.wait_recv()
    scale = 1.0 / (NX * NY * NZ)
    out_ref[...] = unfold((sz[z] + rz[...]) * scale)
    vout_ref[...] = (vz[0] + vz[1]) * scale
    for copy in started + second + last:
        copy.wait_send()


def reduce_grads(grad_w, vectors):
    return pl.pallas_call(
        reduce_kernel,
        out_shape=(
            jax.ShapeDtypeStruct((ROWS_DEV, D), jnp.float32),
            jax.ShapeDtypeStruct((16, 128), jnp.float32),
        ),
        in_specs=[pl.BlockSpec(memory_space=pltpu.VMEM)] * 2,
        out_specs=[pl.BlockSpec(memory_space=pltpu.VMEM)] * 2,
        scratch_shapes=[
            pltpu.VMEM((NX, NY, 16, FOLD), jnp.bfloat16),
            pltpu.VMEM((NX - 1, NY, 16, FOLD), jnp.bfloat16),
            pltpu.VMEM((NY, 16, FOLD), jnp.bfloat16),
            pltpu.VMEM((NY - 1, 16, FOLD), jnp.bfloat16),
            pltpu.VMEM((NY, 16, FOLD), jnp.float32),
            pltpu.VMEM((2, 8, FOLD), jnp.float32),
            pltpu.VMEM((8, FOLD), jnp.float32),
            pltpu.VMEM((NX, 16, 128), jnp.float32),
            pltpu.VMEM((NY, 16, 128), jnp.float32),
            pltpu.VMEM((2, 16, 128), jnp.float32),
            pltpu.SemaphoreType.DMA((NX - 1,)),
            pltpu.SemaphoreType.DMA((NX - 1,)),
            pltpu.SemaphoreType.DMA((NY - 1,)),
            pltpu.SemaphoreType.DMA((NY - 1,)),
            pltpu.SemaphoreType.DMA((2,)),
            pltpu.SemaphoreType.DMA((NX - 1,)),
            pltpu.SemaphoreType.DMA((NX - 1,)),
            pltpu.SemaphoreType.DMA((NY - 1,)),
            pltpu.SemaphoreType.DMA((NY - 1,)),
            pltpu.SemaphoreType.DMA((2,)),
        ],
        compiler_params=pltpu.CompilerParams(
            collective_id=0, has_side_effects=True, vmem_limit_bytes=32 * 1024 * 1024),
        name="reduce_grads",
    )(grad_w, vectors)


def body(
    patches,
    item_counts,
    item_ids,
    block_dest,
    enc_weight,
    enc_bias,
    enc_gain,
    item_bias,
    user_state,
    user_proj,
    positives,
):
    n_enc = lax.axis_size("enc")
    blocks_dev = ITEMS_DEV * BLOCKS_ITEM
    capacity = max(2, (blocks_dev + n_enc - 1) // n_enc)
    slots = n_enc * capacity
    live_items = item_counts[0]
    blocks = patches.reshape(blocks_dev, BLOCK_ROWS * PATCH_IN)
    live_block = jnp.arange(blocks_dev, dtype=jnp.int32) // BLOCKS_ITEM < live_items
    enc_index = jnp.arange(n_enc, dtype=jnp.int32)
    routed = ((block_dest[:, None] == enc_index[None, :]) & live_block[:, None]).astype(jnp.int32)
    rank_slot = jnp.cumsum(routed, axis=0) - routed
    slot_index = jnp.sum(routed * (enc_index[None, :] * capacity + rank_slot), axis=1)
    selector = (
        (jnp.arange(slots, dtype=jnp.int32)[:, None] == slot_index[None, :]) & live_block[None, :]
    ).astype(jnp.bfloat16)
    outgoing = jnp.dot(selector, blocks, preferred_element_type=jnp.float32).astype(jnp.bfloat16)
    outgoing = outgoing.reshape(n_enc, capacity, BLOCK_ROWS, PATCH_IN)
    weight = enc_weight[0]
    bias_vec = enc_bias[0]
    gain_vec = enc_gain[0]
    received = lax.all_to_all(outgoing, "enc", split_axis=0, concat_axis=0, tiled=True)
    projected = jnp.einsum("skrp,pd->skrd", received, weight, preferred_element_type=jnp.float32)
    received, projected = (received, projected)
    pooled_out, backward = jax.vjp(pooled_rows, projected, bias_vec, gain_vec)
    partial_value = pooled_out.astype(jnp.bfloat16)
    returned = lax.all_to_all(partial_value, "enc", split_axis=0, concat_axis=0, tiled=True)
    block_part = jnp.dot(selector.T, returned.reshape(slots, D), preferred_element_type=jnp.float32)
    summed = jnp.sum(block_part.reshape(ITEMS_DEV, BLOCKS_ITEM, D), axis=1)
    embed = (summed / PATCHES).astype(jnp.bfloat16)
    user_vec = jnp.dot(user_state, user_proj, preferred_element_type=jnp.float32).astype(
        jnp.bfloat16
    )
    catalogue = jnp.arange(item_bias.shape[0], dtype=jnp.int32)
    bias_items = jnp.sum(
        jnp.where(item_ids[:, None] == catalogue[None, :], item_bias[None, :], 0.0), axis=1
    )
    scores = (
        jnp.dot(user_vec, embed.T, preferred_element_type=jnp.float32) * score_scale
        + bias_items[None, :]
    )
    item_index = jnp.arange(ITEMS_DEV, dtype=jnp.int32)
    live_item = item_index < live_items
    target = (item_index[None, :] == (positives % live_items)[:, None]).astype(jnp.float32)
    d_score = jnp.where(
        live_item[None, :], loss_weight * (jax.nn.sigmoid(scores) - target), 0.0
    ).astype(jnp.bfloat16)
    d_embed = (
        jnp.dot(d_score.T, user_vec, preferred_element_type=jnp.float32) * score_scale
    ).astype(jnp.bfloat16)
    d_user_vec = (jnp.dot(d_score, embed, preferred_element_type=jnp.float32) * score_scale).astype(
        jnp.bfloat16
    )
    d_user = jnp.dot(d_user_vec, user_proj.T, preferred_element_type=jnp.float32).astype(
        jnp.bfloat16
    )
    d_block = jnp.repeat(d_embed, BLOCKS_ITEM, axis=0)
    grad_out = jnp.dot(selector, d_block, preferred_element_type=jnp.float32).astype(jnp.bfloat16)
    grad_out = grad_out.reshape(n_enc, capacity, D)
    grad_in = lax.all_to_all(grad_out, "enc", split_axis=0, concat_axis=0, tiled=True)
    d_part = grad_in.astype(jnp.float32) / PATCHES
    d_proj, d_bias, d_gain = backward(d_part)
    d_proj_low = d_proj.astype(jnp.bfloat16)
    grad_terms = jnp.einsum(
        "skrp,skrd->pd", received, d_proj_low, preferred_element_type=jnp.float32
    )
    vectors = jnp.concatenate([d_bias, d_gain, jnp.zeros((512,), jnp.float32)]).reshape(16, 128)
    mine, vectors = reduce_grads(grad_terms, vectors)
    flat = vectors.reshape(-1)
    return (d_user, mine[None], flat[None, :D], flat[None, D : 2 * D])


def solution(mesh):
    return jax.shard_map(
        body,
        mesh=mesh,
        in_specs=(
            P(("dp", "enc"), None, None),
            P(("dp", "enc")),
            P(("dp", "enc")),
            P(("dp", "enc")),
            P("enc", None, None),
            P("enc", None),
            P("enc", None),
            P(),
            P(("dp", "enc"), None),
            P(),
            P(("dp", "enc")),
        ),
        out_specs=(P(("dp", "enc"), None), P("enc", "dp", None), P("enc", None), P("enc", None)),
        check_vma=False,
    )
```

```python
import jax
import jax.numpy as jnp
from jax import lax
from jax.experimental import pallas as pl
from jax.experimental.pallas import tpu as pltpu
from jax.sharding import PartitionSpec as P

D = 768
PATCHES = 196
BLOCK_ROWS = 49
BLOCKS_ITEM = 4
ITEMS_DEV = 4
BLOCKS_DEV = ITEMS_DEV * BLOCKS_ITEM
USERS_DEV = 256
CAP = 2
N_ENC = 12
SLOTS = N_ENC * CAP
MAIN = 48
NX, NY, NZ = 4, 8, 2
ROWS_DEV = 12
FOLD = 1152
LANES = 128
PIECES = D // LANES
GROUP = 16

score_scale = 0.1
loss_weight = 16.0
norm_eps = 1e-05
GELU_A = 0.7978845608028654
GELU_B = 0.044715

f32 = jnp.float32
bf16 = jnp.bfloat16


def fold(rows):
    tail = rows[8:12]
    return jnp.concatenate([rows[0:8], jnp.concatenate([tail[:, :384], tail[:, 384:]], axis=0)], axis=1)


def unfold(folded):
    tail = folded[:, 768:]
    return jnp.concatenate([folded[:, :768], jnp.concatenate([tail[0:4], tail[4:8]], axis=1)], axis=0)


def row_to_tile(row):
    pieces = [row[:, c * LANES : (c + 1) * LANES] for c in range(PIECES)]
    return jnp.concatenate(pieces + [jnp.zeros((2, LANES), row.dtype)], axis=0)


def tile_to_row(tile):
    return jnp.concatenate([tile[c : c + 1] for c in range(PIECES)], axis=1)


def sign3(core):
    return 1 - 2 * core


def offset(p, core):
    return ((p + 1) // 2) * (2 * (p % 2) - 1) * (1 + (p // 5) * (sign3(core) - 1))


def normed_rows(projected, bias, gain):
    shifted = projected + bias
    center = jnp.sum(shifted, axis=-1, keepdims=True) * (1.0 / D)
    deviation = shifted - center
    variance = jnp.sum(deviation * deviation, axis=-1, keepdims=True) * (1.0 / D)
    rstd = lax.rsqrt(variance + norm_eps)
    xhat = deviation * rstd
    n = xhat * gain
    square = n * n
    t = jnp.tanh(n * (GELU_A + (GELU_A * GELU_B) * square))
    half = 0.5 + 0.5 * t
    act = n * half
    slope = half + (0.5 * n) * (1.0 - t * t) * (GELU_A + (3.0 * GELU_A * GELU_B) * square)
    return act, slope, xhat, rstd


def rows_back(u, slope, xhat, rstd):
    t = slope * u
    m1 = jnp.sum(t, axis=-1, keepdims=True) * (1.0 / D)
    m2 = jnp.sum(t * xhat, axis=-1, keepdims=True) * (1.0 / D)
    return rstd * (t - m1 - xhat * m2)


def step_kernel(
    src_ref, ids_ref, live_ref, items_ref, chosen_ref, patches_ref, w_ref, bias_ref, gain_ref, ibias_ref,
    users_ref, proj_ref,
    duser_ref, out_ref, bout_ref, gout_ref,
    main, tails, send, recv, tsend, trecv, trows, xtail, psend, precv, dsend, drecv,
    proj, xhat_m, slope_m, rstd_m, act_t, xhat_t, slope_t, rstd_t, dtail, gsum, dlow, dlow_t, uvec, dbacc, g,
    sx, rx, sy, ry, accx, sz, rz, vown, vx, vy, vz,
    sem_s, sem_r, sem_ts, sem_tr, sem_ps, sem_pr, sem_ds, sem_dr,
    sem_sx, sem_rx, sem_sy, sem_ry, sem_z, sem_vsx, sem_vrx, sem_vsy, sem_vry, sem_vz,
):
    dp = lax.axis_index("dp")
    enc = lax.axis_index("enc")
    x = dp // (NY * NZ)
    y = (dp // NZ) % NY
    z = dp % NZ
    core = enc % 2
    ring = z * 6 + enc // 2

    def at(xx, yy, zz):
        return {"dp": (xx * NY + yy) * NZ + zz}

    def on_ring(place, which):
        place = (place + 12) % 12
        return {"dp": (x * NY + y) * NZ + place // 6, "enc": (place % 6) * 2 + which}

    def dest(p, r):
        return on_ring(ring + offset(p, core), (core + r) % 2)

    def source(p, r):
        other = (core + r) % 2
        return on_ring(ring - offset(p, other), other)

    barrier = pltpu.get_barrier_semaphore()
    partners = 0
    for p in range(6):
        for r in range(2):
            if p or r:
                pl.semaphore_signal(barrier, inc=1, device_id=source(p, r))
                partners += 1
    for d in range(1, NX):
        pl.semaphore_signal(barrier, inc=1, device_id=at((x + d) % NX, y, z))
    for d in range(1, NY):
        pl.semaphore_signal(barrier, inc=1, device_id=at(x, (y + d) % NY, z))
    pl.semaphore_signal(barrier, inc=1, device_id=at(x, y, 1 - z))
    partners += NX + NY - 1

    tails[...] = jnp.zeros_like(tails)
    row = lax.broadcasted_iota(jnp.int32, (208, PATCHES), 0)
    col = lax.broadcasted_iota(jnp.int32, (208, PATCHES), 1)
    steps = (row >= 48).astype(jnp.int32) + (row >= 96).astype(jnp.int32) + (row >= 144).astype(jnp.int32)
    origin = jnp.where(row < 192, row + steps, (row - 192) * BLOCK_ROWS + MAIN)
    order = jnp.where(origin == col, 1.0, 0.0).astype(bf16)
    for i in range(ITEMS_DEV):
        sorted_rows = jnp.dot(order, patches_ref[i], preferred_element_type=f32)
        for b in range(BLOCKS_ITEM):
            main[i * BLOCKS_ITEM + b] = sorted_rows[b * MAIN : (b + 1) * MAIN].astype(bf16)
            tails[i * BLOCKS_ITEM + b] = row_to_tile(sorted_rows[192 + b : 193 + b])

    def remote(src, dst, ssem, rsem, device):
        return pltpu.make_async_remote_copy(
            src_ref=src, dst_ref=dst, send_sem=ssem, recv_sem=rsem, device_id=device)

    def tail_tile(j):
        return jnp.concatenate([tails[src_ref[2 * j]], tails[src_ref[2 * j + 1]]], axis=0).astype(bf16)

    trecv[0] = tail_tile(0)
    for j in range(1, N_ENC):
        tsend[j] = tail_tile(j)
    pl.semaphore_wait(barrier, partners)
    started = []

    def start(copy):
        copy.start()
        started.append(copy)
        return copy

    for j in range(1, N_ENC):
        start(remote(tsend.at[j], trecv.at[j], sem_ts.at[j], sem_tr.at[j], dest(j // 2, j % 2)))
    for p in (5, 4, 3, 2, 1, 0):
        for r in range(2):
            j = 2 * p + r
            if j:
                for k in range(CAP):
                    send[j, k] = main[src_ref[2 * j + k]]
                start(remote(send.at[j], recv.at[j], sem_s.at[j], sem_r.at[j], dest(p, r)))
    for k in range(CAP):
        recv[0, k] = main[src_ref[k]]

    @pl.loop(0, D // 256)
    def _(m):
        first = pl.multiple_of(m * 256, 256)
        uvec[:, pl.ds(first, 256)] = jnp.dot(
            users_ref[...], proj_ref[:, pl.ds(first, 256)], preferred_element_type=f32).astype(bf16)

    entry = lax.broadcasted_iota(jnp.int32, (512, LANES), 0) * LANES + lax.broadcasted_iota(jnp.int32, (512, LANES), 1)
    item_row = lax.broadcasted_iota(jnp.int32, (8, 1), 0)
    item_biases = jnp.zeros((8, 1), f32)
    for i in range(ITEMS_DEV):
        picked = jnp.where(entry == ids_ref[i], ibias_ref[...], 0.0)
        picked = jnp.sum(jnp.sum(picked, axis=0, keepdims=True), axis=1, keepdims=True)
        item_biases = item_biases + jnp.where(item_row == i, picked, 0.0)

    out_row = lax.broadcasted_iota(jnp.int32, (48, N_ENC * 16), 0)
    in_col = lax.broadcasted_iota(jnp.int32, (48, N_ENC * 16), 1)
    belongs = ((out_row & 7) == items_ref[...]) & ((out_row >> 3) == (in_col & 7))
    belongs = jnp.where(belongs, 1.0, 0.0).astype(bf16)

    bias = bias_ref[...]
    gain = gain_ref[...]

    trows[...] = jnp.zeros_like(trows)
    for j in range(N_ENC):
        if j:
            remote(tsend.at[j], trecv.at[j], sem_ts.at[j], sem_tr.at[j], dest(j // 2, j % 2)).wait_recv()
        tile = trecv[j].astype(f32)
        for k in range(CAP):
            trows[2 * j + k : 2 * j + k + 1, :] = tile_to_row(tile[8 * k : 8 * k + 8])
    xtail[...] = trows[...].astype(bf16)
    proj[0:32, :] = jnp.dot(xtail[...], w_ref[...], preferred_element_type=f32)
    for s in range(2):
        rows = slice(s * GROUP, (s + 1) * GROUP)
        act, slope, xhat, rstd = normed_rows(proj[rows, :], bias, gain)
        act_t[rows, :] = act
        slope_t[rows, :] = slope
        xhat_t[rows, :] = xhat
        rstd_t[rows, :] = jnp.broadcast_to(rstd, (GROUP, LANES))

    def forward(q, carry):
        p = (6 - q) % 6
        for r in range(2):
            @pl.when(2 * p + r > 0)
            def _():
                remote(send.at[2 * p + r], recv.at[2 * p + r], sem_s.at[2 * p + r], sem_r.at[2 * p + r],
                       {"enc": (enc // 2) * 2 + 1 - core}).wait_recv()
        @pl.loop(0, D // 256)
        def _(m):
            first = pl.multiple_of(m * 256, 256)
            proj[:, pl.ds(first, 256)] = jnp.dot(
                recv[pl.ds(2 * p, 2)].reshape(4 * MAIN, D), w_ref[:, pl.ds(first, 256)], preferred_element_type=f32)

        def slot(s, carry):
            own = 4 * p + s
            pooled = act_t[pl.ds(own, 1), :]
            weighted = slope_t[pl.ds(own, 1), :] * xhat_t[pl.ds(own, 1), :]
            pool, gs = None, None
            for m in range(MAIN // GROUP):
                act, slope, xhat, rstd = normed_rows(
                    proj[pl.ds(pl.multiple_of(s * MAIN + m * GROUP, GROUP), GROUP), :], bias, gain)
                rows = slice(m * GROUP, (m + 1) * GROUP)
                slope_m[own, rows, :] = slope
                xhat_m[own, rows, :] = xhat
                rstd_m[own, rows, :] = jnp.broadcast_to(rstd, (GROUP, LANES))
                product = slope * xhat
                act = act[0:8] + act[8:16]
                product = product[0:8] + product[8:16]
                pool = act if pool is None else pool + act
                gs = product if gs is None else gs + product
            gsum[pl.ds(own, 1), :] = jnp.sum(gs, axis=0, keepdims=True) + weighted
            trows[pl.ds(own, 1), :] = jnp.sum(pool, axis=0, keepdims=True) + pooled
            return carry
        lax.fori_loop(0, 4, slot, 0)
        for r in range(2):
            j = 2 * p + r
            tile = jnp.concatenate(
                [row_to_tile(trows[pl.ds(2 * j + k, 1), :]) for k in range(CAP)], axis=0).astype(bf16)
            psend[j] = tile
            if r == 0:
                @pl.when(p == 0)
                def _():
                    precv[0] = tile

            @pl.when(j > 0)
            def _():
                remote(psend.at[j], precv.at[j], sem_ps.at[j], sem_pr.at[j], source(p, r)).start()
        return carry
    lax.fori_loop(0, 6, forward, 0)

    returned = [remote(psend.at[j], precv.at[j], sem_ps.at[j], sem_pr.at[j], source(j // 2, j % 2)) for j in range(1, N_ENC)]
    for copy in returned:
        copy.wait_recv()
    summed = jnp.dot(belongs, precv[...].reshape(N_ENC * 16, LANES), preferred_element_type=f32)
    embed = jnp.concatenate([summed[8 * c : 8 * c + 8] for c in range(PIECES)], axis=1)
    embed = (embed / PATCHES).astype(bf16)
    scores = lax.dot_general(embed, uvec[...], (((1,), (1,)), ((), ())), preferred_element_type=f32)
    scores = scores * score_scale + item_biases
    index = lax.broadcasted_iota(jnp.int32, (8, USERS_DEV), 0)
    target = jnp.where(index == chosen_ref[...], 1.0, 0.0)
    sigmoid = 1.0 / (1.0 + jnp.exp(-scores))
    d_score = jnp.where(index < live_ref[0], loss_weight * (sigmoid - target), 0.0).astype(bf16)
    d_embed = jnp.dot(d_score, uvec[...], preferred_element_type=f32) * score_scale
    d_folded = jnp.concatenate([d_embed[:, c * LANES : (c + 1) * LANES] for c in range(PIECES)], axis=0).astype(bf16)
    d_slots = lax.dot_general(belongs, d_folded, (((0,), (0,)), ((), ())), preferred_element_type=f32)
    dsend[...] = d_slots.astype(bf16).reshape(N_ENC, 16, LANES)
    for p in (5, 4, 3, 2, 1, 0):
        for r in range(2):
            j = 2 * p + r
            if j:
                start(remote(dsend.at[j], drecv.at[j], sem_ds.at[j], sem_dr.at[j], dest(p, r)))
    drecv[0] = dsend[0]
    d_user_vec = lax.dot_general(d_score, embed, (((0,), (0,)), ((), ())), preferred_element_type=f32)
    uvec[...] = (d_user_vec * score_scale).astype(bf16)

    @pl.loop(0, D // 256)
    def _(m):
        first = pl.multiple_of(m * 256, 256)
        duser_ref[:, pl.ds(first, 256)] = lax.dot_general(
            uvec[...], proj_ref[pl.ds(first, 256), :], (((1,), (1,)), ((), ())), preferred_element_type=f32).astype(bf16)

    dtail[...] = jnp.zeros_like(dtail)
    dbacc[...] = jnp.zeros_like(dbacc)

    def backward(j, carry):
        @pl.when(j > 0)
        def _():
            remote(dsend.at[j], drecv.at[j], sem_ds.at[j], sem_dr.at[j],
                   {"enc": (enc // 2) * 2 + 1 - core}).wait_recv()
        tile = drecv[j].astype(f32) / PATCHES
        for k in range(CAP):
            own = 2 * j + k
            d_row = tile_to_row(tile[8 * k : 8 * k + 8])
            dtail[pl.ds(own, 1), :] = d_row
            u = d_row * gain
            for m in range(MAIN // GROUP):
                rows = slice(m * GROUP, (m + 1) * GROUP)
                rstd = jnp.concatenate([rstd_m[own, rows, :]] * PIECES, axis=1)
                d_projected = rows_back(u, slope_m[own, rows, :], xhat_m[own, rows, :], rstd)
                dlow[own, rows, :] = d_projected.astype(bf16)
                dbacc[...] += d_projected[0:8] + d_projected[8:16]
        return carry
    lax.fori_loop(0, N_ENC, backward, 0)
    for s in range(2):
        rows = slice(s * GROUP, (s + 1) * GROUP)
        rstd = jnp.concatenate([rstd_t[rows, :]] * PIECES, axis=1)
        d_projected = rows_back(dtail[rows, :] * gain, slope_t[rows, :], xhat_t[rows, :], rstd)
        dlow_t[rows, :] = d_projected.astype(bf16)
        dbacc[...] += d_projected[0:8] + d_projected[8:16]
    d_bias = jnp.sum(dbacc[...], axis=0, keepdims=True)
    d_gain = jnp.sum(dtail[0:SLOTS, :] * gsum[0:SLOTS, :], axis=0, keepdims=True)
    vectors = jnp.concatenate([row_to_tile(d_bias), row_to_tile(d_gain)], axis=0)

    @pl.loop(0, D // 256)
    def _(m):
        first = pl.multiple_of(m * 256, 256)
        g[pl.ds(first, 256), :] = lax.dot_general(
            recv[:, :, :, pl.ds(first, 256)].reshape(SLOTS * MAIN, 256), dlow[...].reshape(SLOTS * MAIN, D),
            (((0,), (0,)), ((), ())), preferred_element_type=f32) + lax.dot_general(
            xtail[:, pl.ds(first, 256)], dlow_t[...], (((0,), (0,)), ((), ())), preferred_element_type=f32)

    for copy in started + returned:
        copy.wait_send()

    vown[...] = vectors

    def pack(xx):
        @pl.loop(0, NY)
        def _(k):
            first = pl.multiple_of((xx * NY + k) * 24, 8)
            chunk = g[pl.ds(first, 24), :]
            sx[xx, k] = jnp.concatenate([fold(chunk[0:12]), fold(chunk[12:24])], axis=0).astype(bf16)

    vx[x] = vectors
    firsts = []
    for d in range(1, NX):
        to = (x + d) % NX
        pack(to)
        firsts.append(remote(sx.at[to], rx.at[d - 1], sem_sx.at[d - 1], sem_rx.at[d - 1], at(to, y, z)))
        firsts.append(remote(vown, vx.at[x], sem_vsx.at[d - 1], sem_vrx.at[d - 1], at(to, y, z)))
        firsts[-2].start()
        firsts[-1].start()
    pack(x)
    for copy in firsts:
        copy.wait_recv()
    vy[y] = (vx[0] + vx[1]) + (vx[2] + vx[3])

    def sum_x(k, carry):
        total = (sx[x, k].astype(f32) + rx[0, k].astype(f32)) + (rx[1, k].astype(f32) + rx[2, k].astype(f32))
        accx[k] = total
        sy[k] = total.astype(bf16)
        return carry
    lax.fori_loop(0, NY, sum_x, 0)
    second = []
    for d in range(1, NY):
        to = (y + d) % NY
        second.append(remote(sy.at[to], ry.at[d - 1], sem_sy.at[d - 1], sem_ry.at[d - 1], at(x, to, z)))
        second.append(remote(vy.at[y], vy.at[y], sem_vsy.at[d - 1], sem_vry.at[d - 1], at(x, to, z)))
        second[-2].start()
        second[-1].start()
    total = accx[y]
    for d in range(1, NY):
        second[2 * d - 2].wait_recv()
        total = total + ry[d - 1].astype(f32)
    for d in range(1, NY):
        second[2 * d - 1].wait_recv()
    vz[0] = ((vy[0] + vy[1]) + (vy[2] + vy[3])) + ((vy[4] + vy[5]) + (vy[6] + vy[7]))
    sz[0] = total[0:8]
    sz[1] = total[8:16]
    last = [
        remote(sz.at[1 - z], rz, sem_z.at[0], sem_z.at[1], at(x, y, 1 - z)),
        remote(vz.at[0], vz.at[1], sem_vz.at[0], sem_vz.at[1], at(x, y, 1 - z)),
    ]
    for copy in last:
        copy.start()
    for copy in last:
        copy.wait_recv()
    scale = 1.0 / (NX * NY * NZ)
    out_ref[...] = unfold((sz[z] + rz[...]) * scale)
    folded = (vz[0] + vz[1]) * scale
    bout_ref[...] = tile_to_row(folded[0:8])
    gout_ref[...] = tile_to_row(folded[8:16])
    for copy in firsts + second + last:
        copy.wait_send()


def train_step(src, ids, live, items, chosen, patches, weight, bias, gain, item_bias, users, proj):
    vmem = pl.BlockSpec(memory_space=pltpu.VMEM)
    smem = pl.BlockSpec(memory_space=pltpu.SMEM)
    dma = pltpu.SemaphoreType.DMA
    return pl.pallas_call(
        step_kernel,
        out_shape=(
            jax.ShapeDtypeStruct((USERS_DEV, D), bf16),
            jax.ShapeDtypeStruct((ROWS_DEV, D), f32),
            jax.ShapeDtypeStruct((1, D), f32),
            jax.ShapeDtypeStruct((1, D), f32),
        ),
        in_specs=[smem] * 3 + [vmem] * 9,
        out_specs=[vmem] * 4,
        scratch_shapes=[
            pltpu.VMEM((BLOCKS_DEV, MAIN, D), bf16),
            pltpu.VMEM((BLOCKS_DEV, 8, LANES), f32),
            pltpu.VMEM((N_ENC, CAP, MAIN, D), bf16),
            pltpu.VMEM((N_ENC, CAP, MAIN, D), bf16),
        ] + [pltpu.VMEM((N_ENC, 16, LANES), bf16)] * 2 + [
            pltpu.VMEM((32, D), f32),
            pltpu.VMEM((32, D), bf16),
        ] + [pltpu.VMEM((N_ENC, 16, LANES), bf16)] * 4 + [
            pltpu.VMEM((4 * MAIN, D), f32),
            pltpu.VMEM((SLOTS, MAIN, D), f32),
            pltpu.VMEM((SLOTS, MAIN, D), f32),
            pltpu.VMEM((SLOTS, MAIN, LANES), f32),
            pltpu.VMEM((32, D), f32),
            pltpu.VMEM((32, D), f32),
            pltpu.VMEM((32, D), f32),
            pltpu.VMEM((32, LANES), f32),
            pltpu.VMEM((32, D), f32),
            pltpu.VMEM((32, D), f32),
            pltpu.VMEM((SLOTS, MAIN, D), bf16),
            pltpu.VMEM((32, D), bf16),
            pltpu.VMEM((USERS_DEV, D), bf16),
            pltpu.VMEM((8, D), f32),
            pltpu.VMEM((D, D), f32),
            pltpu.VMEM((NX, NY, 16, FOLD), bf16),
            pltpu.VMEM((NX - 1, NY, 16, FOLD), bf16),
            pltpu.VMEM((NY, 16, FOLD), bf16),
            pltpu.VMEM((NY - 1, 16, FOLD), bf16),
            pltpu.VMEM((NY, 16, FOLD), f32),
            pltpu.VMEM((2, 8, FOLD), f32),
            pltpu.VMEM((8, FOLD), f32),
            pltpu.VMEM((16, LANES), f32),
            pltpu.VMEM((NX, 16, LANES), f32),
            pltpu.VMEM((NY, 16, LANES), f32),
            pltpu.VMEM((2, 16, LANES), f32),
        ] + [dma((N_ENC,))] * 8 + [
            dma((NX - 1,)), dma((NX - 1,)), dma((NY - 1,)), dma((NY - 1,)), dma((2,)),
            dma((NX - 1,)), dma((NX - 1,)), dma((NY - 1,)), dma((NY - 1,)), dma((2,)),
        ],
        compiler_params=pltpu.CompilerParams(
            collective_id=0, has_side_effects=True, vmem_limit_bytes=48 * 1024 * 1024),
        name="train_step",
    )(src, ids, live, items, chosen, patches, weight, bias, gain, item_bias, users, proj)


def body(
    patches,
    item_counts,
    item_ids,
    block_dest,
    enc_weight,
    enc_bias,
    enc_gain,
    item_bias,
    user_state,
    user_proj,
    positives,
):
    enc = lax.axis_index("enc")
    core = enc % 2
    live_items = item_counts[0]
    place = jnp.arange(N_ENC, dtype=jnp.int32)
    chip = (enc // 2 + offset(place // 2, core) + 6) % 6
    expert = chip * 2 + (core + place % 2) % 2
    number = jnp.arange(BLOCKS_DEV, dtype=jnp.int32)
    live_block = number // BLOCKS_ITEM < live_items
    routed = (block_dest[None, :] == expert[:, None]) & live_block[None, :]
    earlier = (block_dest[None, :] == block_dest[:, None]) & (number[None, :] < number[:, None])
    second = jnp.any(earlier, axis=1)
    taken = jnp.stack([routed & ~second[None, :], routed & second[None, :]], axis=1).astype(jnp.int32)
    src = jnp.sum(taken * number[None, None, :], axis=2).reshape(-1)
    present = jnp.sum(taken, axis=2).reshape(-1)
    item = jnp.where(present > 0, src // BLOCKS_ITEM, -1)
    items = jnp.broadcast_to(item[:, None], (SLOTS, 8)).reshape(1, SLOTS * 8)
    chosen = (positives % live_items)[None, :]
    d_user, mine, d_bias, d_gain = train_step(
        src, item_ids, item_counts, items, chosen, patches, enc_weight[0], enc_bias, enc_gain,
        item_bias.reshape(-1, LANES), user_state, user_proj)
    return (d_user, mine[None], d_bias, d_gain)


def solution(mesh):
    return jax.shard_map(
        body,
        mesh=mesh,
        in_specs=(
            P(("dp", "enc"), None, None),
            P(("dp", "enc")),
            P(("dp", "enc")),
            P(("dp", "enc")),
            P("enc", None, None),
            P("enc", None),
            P("enc", None),
            P(),
            P(("dp", "enc"), None),
            P(),
            P(("dp", "enc")),
        ),
        out_specs=(P(("dp", "enc"), None), P("enc", "dp", None), P("enc", None), P("enc", None)),
        check_vma=False,
    )
```

```python
import jax
import jax.numpy as jnp
from jax import lax
from jax.experimental import pallas as pl
from jax.experimental.pallas import tpu as pltpu
from jax.sharding import PartitionSpec as P

D = 768
PATCHES = 196
BLOCK_ROWS = 49
BLOCKS_ITEM = 4
ITEMS_DEV = 4
BLOCKS_DEV = ITEMS_DEV * BLOCKS_ITEM
USERS_DEV = 256
CAP = 2
N_ENC = 12
SLOTS = N_ENC * CAP
MAIN = 48
NX, NY, NZ = 4, 8, 2
ROWS_DEV = 12
PIECE = 256
N_PIECES = D // PIECE
FOLD = 384
LANES = 128
PIECES = D // LANES
GROUP = 16

score_scale = 0.1
loss_weight = 16.0
norm_eps = 1e-05
GELU_A = 0.7978845608028654
GELU_B = 0.044715

f32 = jnp.float32
bf16 = jnp.bfloat16


def fold(rows):
    tail = rows[8:12]
    return jnp.concatenate([rows[0:8], jnp.concatenate([tail[:, :LANES], tail[:, LANES:]], axis=0)], axis=1)


def unfold(folded):
    tail = folded[:, PIECE:]
    return jnp.concatenate([folded[:, :PIECE], jnp.concatenate([tail[0:4], tail[4:8]], axis=1)], axis=0)


def row_to_tile(row):
    pieces = [row[:, c * LANES : (c + 1) * LANES] for c in range(PIECES)]
    return jnp.concatenate(pieces + [jnp.zeros((2, LANES), row.dtype)], axis=0)


def tile_to_row(tile):
    return jnp.concatenate([tile[c : c + 1] for c in range(PIECES)], axis=1)


def sign3(core):
    return 1 - 2 * core


def offset(p, core):
    return ((p + 1) // 2) * (2 * (p % 2) - 1) * (1 + (p // 5) * (sign3(core) - 1))


def normed_rows(projected, bias, gain):
    shifted = projected + bias
    center = jnp.sum(shifted, axis=-1, keepdims=True) * (1.0 / D)
    deviation = shifted - center
    variance = jnp.sum(deviation * deviation, axis=-1, keepdims=True) * (1.0 / D)
    rstd = lax.rsqrt(variance + norm_eps)
    xhat = deviation * rstd
    n = xhat * gain
    square = n * n
    t = jnp.tanh(n * (GELU_A + (GELU_A * GELU_B) * square))
    half = 0.5 + 0.5 * t
    act = n * half
    slope = half + (0.5 * n) * (1.0 - t * t) * (GELU_A + (3.0 * GELU_A * GELU_B) * square)
    return act, slope, xhat, rstd


def rows_back(u, slope, xhat, rstd):
    t = slope * u
    m1 = jnp.sum(t, axis=-1, keepdims=True) * (1.0 / D)
    m2 = jnp.sum(t * xhat, axis=-1, keepdims=True) * (1.0 / D)
    return rstd * (t - m1 - xhat * m2)


def step_kernel(
    blocks_ref, ids_ref, live_ref, positives_ref, patches_ref, w_hbm, bias_ref, gain_ref, ibias_hbm,
    users_hbm, proj_hbm,
    duser_ref, out_ref, bout_ref, gout_ref,
    main, tails, send, recv, tsend, trecv, trows, xtail, psend, precv, dsend, drecv,
    proj, xhat_m, slope_m, rstd_m, act_t, xhat_t, slope_t, rstd_t, dtail, gsum, dlow, dlow_t, uvec, dbacc, g,
    w_ref, ibias_ref, users_ref, proj_ref, proj_t, xt, xt_t,
    sx, rx, relay, sy, ry, accx, sz, rz, vown, vx, vy, vz,
    sem_s, sem_r, sem_ts, sem_tr, sem_ps, sem_pr, sem_ds, sem_dr,
    sem_sx, sem_rx, sem_sy, sem_ry, sem_z, sem_vsx, sem_vrx, sem_vsy, sem_vry, sem_vz, sem_load,
):
    dp = lax.axis_index("dp")
    enc = lax.axis_index("enc")
    x = dp // (NY * NZ)
    y = (dp // NZ) % NY
    z = dp % NZ
    core = enc % 2
    ring = z * 6 + enc // 2

    def at(xx, yy, zz):
        return {"dp": (xx * NY + yy) * NZ + zz}

    def on_ring(place, which):
        place = (place + 12) % 12
        return {"dp": (x * NY + y) * NZ + place // 6, "enc": (place % 6) * 2 + which}

    def dest(p, r):
        return on_ring(ring + offset(p, core), (core + r) % 2)

    def source(p, r):
        other = (core + r) % 2
        return on_ring(ring - offset(p, other), other)

    loads = [
        pltpu.make_async_copy(there, here, sem_load.at[n])
        for n, (there, here) in enumerate(
            [(users_hbm, users_ref), (proj_hbm, proj_ref), (ibias_hbm, ibias_ref), (w_hbm, w_ref)])
    ]
    barrier = pltpu.get_barrier_semaphore()
    partners = 0
    for p in range(6):
        for r in range(2):
            if p or r:
                pl.semaphore_signal(barrier, inc=1, device_id=source(p, r))
                partners += 1
    for d in range(1, NX):
        pl.semaphore_signal(barrier, inc=1, device_id=at((x + d) % NX, y, z))
    for d in range(1, NY):
        pl.semaphore_signal(barrier, inc=1, device_id=at(x, (y + d) % NY, z))
    pl.semaphore_signal(barrier, inc=1, device_id=at(x, y, 1 - z))
    partners += NX + NY - 1
    for load in loads:
        load.start()

    n_live = live_ref[0] * BLOCKS_ITEM
    named = [jnp.where(b < n_live, blocks_ref[b], -1) for b in range(BLOCKS_DEV)]
    src = []
    lane_slot = lax.broadcasted_iota(jnp.int32, (1, N_ENC * 16), 1) >> 3
    items = jnp.full((1, N_ENC * 16), -1, jnp.int32)
    for j in range(N_ENC):
        expert = dest(j // 2, j % 2)["enc"]
        low, high = jnp.int32(BLOCKS_DEV), jnp.int32(-1)
        for b in range(BLOCKS_DEV):
            high = jnp.where(named[b] == expert, b, high)
            back = BLOCKS_DEV - 1 - b
            low = jnp.where(named[back] == expert, back, low)
        src.append(jnp.minimum(low, BLOCKS_DEV - 1))
        src.append(jnp.maximum(high, 0))
        items = jnp.where(lane_slot == 2 * j, jnp.where(low < BLOCKS_DEV, low >> 2, -1), items)
        items = jnp.where(lane_slot == 2 * j + 1, jnp.where(high > low, high >> 2, -1), items)

    tails[...] = jnp.zeros_like(tails)
    row = lax.broadcasted_iota(jnp.int32, (208, PATCHES), 0)
    col = lax.broadcasted_iota(jnp.int32, (208, PATCHES), 1)
    steps = (row >= 48).astype(jnp.int32) + (row >= 96).astype(jnp.int32) + (row >= 144).astype(jnp.int32)
    origin = jnp.where(row < 192, row + steps, (row - 192) * BLOCK_ROWS + MAIN)
    order = jnp.where(origin == col, 1.0, 0.0).astype(bf16)
    for i in range(ITEMS_DEV):
        sorted_rows = jnp.dot(order, patches_ref[:, i, :], preferred_element_type=f32)
        for b in range(BLOCKS_ITEM):
            main[i * BLOCKS_ITEM + b] = sorted_rows[b * MAIN : (b + 1) * MAIN].astype(bf16)
            tails[i * BLOCKS_ITEM + b] = row_to_tile(sorted_rows[192 + b : 193 + b])

    def remote(src, dst, ssem, rsem, device):
        return pltpu.make_async_remote_copy(
            src_ref=src, dst_ref=dst, send_sem=ssem, recv_sem=rsem, device_id=device)

    def tail_tile(j):
        return jnp.concatenate([tails[src[2 * j]], tails[src[2 * j + 1]]], axis=0).astype(bf16)

    trecv[0] = tail_tile(0)
    for j in range(1, N_ENC):
        tsend[j] = tail_tile(j)
    pl.semaphore_wait(barrier, partners)
    started = []

    def start(copy):
        copy.start()
        started.append(copy)
        return copy

    for j in range(1, N_ENC):
        start(remote(tsend.at[j], trecv.at[j], sem_ts.at[j], sem_tr.at[j], dest(j // 2, j % 2)))
    for p in (5, 4, 3, 2, 1, 0):
        for r in range(2):
            j = 2 * p + r
            if j:
                for k in range(CAP):
                    send[j, k] = main[src[2 * j + k]]
                start(remote(send.at[j], recv.at[j], sem_s.at[j], sem_r.at[j], dest(p, r)))
    for k in range(CAP):
        recv[0, k] = main[src[k]]

    for load in loads:
        load.wait()

    @pl.loop(0, D // 256)
    def _(m):
        first = pl.multiple_of(m * 256, 256)
        uvec[:, pl.ds(first, 256)] = jnp.dot(
            users_ref[...], proj_ref[:, pl.ds(first, 256)], preferred_element_type=f32).astype(bf16)

    @pl.loop(0, PIECES)
    def _(c):
        lanes = pl.ds(pl.multiple_of(c * LANES, LANES), LANES)
        proj_t[lanes, :] = proj_ref[:, lanes].T

    entry = lax.broadcasted_iota(jnp.int32, (512, LANES), 0) * LANES + lax.broadcasted_iota(jnp.int32, (512, LANES), 1)
    item_row = lax.broadcasted_iota(jnp.int32, (8, 1), 0)
    item_biases = jnp.zeros((8, 1), f32)
    for i in range(ITEMS_DEV):
        picked = jnp.where(entry == ids_ref[i], ibias_ref[...], 0.0)
        picked = jnp.sum(jnp.sum(picked, axis=0, keepdims=True), axis=1, keepdims=True)
        item_biases = item_biases + jnp.where(item_row == i, picked, 0.0)

    out_row = lax.broadcasted_iota(jnp.int32, (48, N_ENC * 16), 0)
    in_col = lax.broadcasted_iota(jnp.int32, (48, N_ENC * 16), 1)
    belongs = ((out_row & 7) == items) & ((out_row >> 3) == (in_col & 7))
    belongs = jnp.where(belongs, 1.0, 0.0).astype(bf16)

    bias = bias_ref[...]
    gain = gain_ref[...]

    trows[...] = jnp.zeros_like(trows)
    for j in range(N_ENC):
        if j:
            remote(tsend.at[j], trecv.at[j], sem_ts.at[j], sem_tr.at[j], dest(j // 2, j % 2)).wait_recv()
        tile = trecv[j].astype(f32)
        for k in range(CAP):
            trows[2 * j + k : 2 * j + k + 1, :] = tile_to_row(tile[8 * k : 8 * k + 8])
    xtail[...] = trows[...].astype(bf16)
    xt_t[...] = trows[...].T.astype(bf16)
    proj[0:32, :] = jnp.dot(xtail[...], w_ref[...], preferred_element_type=f32)
    for s in range(2):
        rows = slice(s * GROUP, (s + 1) * GROUP)
        act, slope, xhat, rstd = normed_rows(proj[rows, :], bias, gain)
        act_t[rows, :] = act
        slope_t[rows, :] = slope
        xhat_t[rows, :] = xhat
        rstd_t[rows, :] = jnp.broadcast_to(rstd, (GROUP, LANES))

    def forward(q, carry):
        p = (6 - q) % 6
        for r in range(2):
            @pl.when(2 * p + r > 0)
            def _():
                remote(send.at[2 * p + r], recv.at[2 * p + r], sem_s.at[2 * p + r], sem_r.at[2 * p + r],
                       {"enc": (enc // 2) * 2 + 1 - core}).wait_recv()
        @pl.loop(0, D // 256)
        def _(m):
            first = pl.multiple_of(m * 256, 256)
            proj[:, pl.ds(first, 256)] = jnp.dot(
                recv[pl.ds(2 * p, 2)].reshape(4 * MAIN, D), w_ref[:, pl.ds(first, 256)], preferred_element_type=f32)

        def slot(s, carry):
            own = 4 * p + s
            pooled = act_t[pl.ds(own, 1), :]
            weighted = slope_t[pl.ds(own, 1), :] * xhat_t[pl.ds(own, 1), :]
            pool, gs = None, None
            for m in range(MAIN // GROUP):
                act, slope, xhat, rstd = normed_rows(
                    proj[pl.ds(pl.multiple_of(s * MAIN + m * GROUP, GROUP), GROUP), :], bias, gain)
                rows = slice(m * GROUP, (m + 1) * GROUP)
                slope_m[own, rows, :] = slope
                xhat_m[own, rows, :] = xhat
                rstd_m[own, rows, :] = jnp.broadcast_to(rstd, (GROUP, LANES))
                product = slope * xhat
                act = act[0:8] + act[8:16]
                product = product[0:8] + product[8:16]
                pool = act if pool is None else pool + act
                gs = product if gs is None else gs + product
            gsum[pl.ds(own, 1), :] = jnp.sum(gs, axis=0, keepdims=True) + weighted
            trows[pl.ds(own, 1), :] = jnp.sum(pool, axis=0, keepdims=True) + pooled
            return carry
        lax.fori_loop(0, 4, slot, 0)
        for r in range(2):
            j = 2 * p + r
            tile = jnp.concatenate(
                [row_to_tile(trows[pl.ds(2 * j + k, 1), :]) for k in range(CAP)], axis=0).astype(bf16)
            psend[j] = tile
            if r == 0:
                @pl.when(p == 0)
                def _():
                    precv[0] = tile

            @pl.when(j > 0)
            def _():
                remote(psend.at[j], precv.at[j], sem_ps.at[j], sem_pr.at[j], source(p, r)).start()
        return carry
    lax.fori_loop(0, 6, forward, 0)

    returned = [remote(psend.at[j], precv.at[j], sem_ps.at[j], sem_pr.at[j], source(j // 2, j % 2)) for j in range(1, N_ENC)]

    def turn(c, carry):
        lanes = pl.ds(pl.multiple_of(c * LANES, LANES), LANES)
        xt[lanes, :] = recv[:, :, :, lanes].reshape(SLOTS * MAIN, LANES).T
        return carry
    lax.fori_loop(0, PIECES // 2, turn, 0)
    for copy in returned:
        copy.wait_recv()
    summed = jnp.dot(belongs, precv[...].reshape(N_ENC * 16, LANES), preferred_element_type=f32)
    embed = jnp.concatenate([summed[8 * c : 8 * c + 8] for c in range(PIECES)], axis=1)
    embed = (embed / PATCHES).astype(bf16)
    scores = lax.dot_general(embed, uvec[...], (((1,), (1,)), ((), ())), preferred_element_type=f32)
    scores = scores * score_scale + item_biases
    index = lax.broadcasted_iota(jnp.int32, (8, USERS_DEV), 0)
    chosen = positives_ref[...].astype(f32)
    chosen = jnp.concatenate([chosen[0:1], chosen[1:2]], axis=1)
    live = live_ref[0].astype(f32)
    chosen = chosen - live * jnp.floor((chosen + 0.5) / live)
    target = jnp.where(index.astype(f32) == chosen, 1.0, 0.0)
    sigmoid = 1.0 / (1.0 + jnp.exp(-scores))
    d_score = jnp.where(index < live_ref[0], loss_weight * (sigmoid - target), 0.0).astype(bf16)
    d_embed = jnp.dot(d_score, uvec[...], preferred_element_type=f32) * score_scale
    d_folded = jnp.concatenate([d_embed[:, c * LANES : (c + 1) * LANES] for c in range(PIECES)], axis=0).astype(bf16)
    d_slots = lax.dot_general(belongs, d_folded, (((0,), (0,)), ((), ())), preferred_element_type=f32)
    dsend[...] = d_slots.astype(bf16).reshape(N_ENC, 16, LANES)
    for p in (5, 4, 3, 2, 1, 0):
        for r in range(2):
            j = 2 * p + r
            if j:
                start(remote(dsend.at[j], drecv.at[j], sem_ds.at[j], sem_dr.at[j], dest(p, r)))
    drecv[0] = dsend[0]
    lax.fori_loop(PIECES // 2, PIECES, turn, 0)

    dtail[...] = jnp.zeros_like(dtail)
    dbacc[...] = jnp.zeros_like(dbacc)

    def backward(j, carry):
        @pl.when(j > 0)
        def _():
            remote(dsend.at[j], drecv.at[j], sem_ds.at[j], sem_dr.at[j],
                   {"enc": (enc // 2) * 2 + 1 - core}).wait_recv()
        tile = drecv[j].astype(f32) / PATCHES
        for k in range(CAP):
            own = 2 * j + k
            d_row = tile_to_row(tile[8 * k : 8 * k + 8])
            dtail[pl.ds(own, 1), :] = d_row
            u = d_row * gain
            for m in range(MAIN // GROUP):
                rows = slice(m * GROUP, (m + 1) * GROUP)
                rstd = jnp.concatenate([rstd_m[own, rows, :]] * PIECES, axis=1)
                d_projected = rows_back(u, slope_m[own, rows, :], xhat_m[own, rows, :], rstd)
                dlow[own, rows, :] = d_projected.astype(bf16)
                dbacc[...] += d_projected[0:8] + d_projected[8:16]
        return carry
    lax.fori_loop(0, N_ENC, backward, 0)
    for s in range(2):
        rows = slice(s * GROUP, (s + 1) * GROUP)
        rstd = jnp.concatenate([rstd_t[rows, :]] * PIECES, axis=1)
        d_projected = rows_back(dtail[rows, :] * gain, slope_t[rows, :], xhat_t[rows, :], rstd)
        dlow_t[rows, :] = d_projected.astype(bf16)
        dbacc[...] += d_projected[0:8] + d_projected[8:16]
    d_bias = jnp.sum(dbacc[...], axis=0, keepdims=True)
    d_gain = jnp.sum(dtail[0:SLOTS, :] * gsum[0:SLOTS, :], axis=0, keepdims=True)
    vectors = jnp.concatenate([row_to_tile(d_bias), row_to_tile(d_gain)], axis=0)

    vown[...] = vectors
    vx[x] = vectors
    vectors_x = [remote(vown, vx.at[x], sem_vsx.at[d - 1], sem_vrx.at[d - 1], at((x + d) % NX, y, z)) for d in range(1, NX)]
    for copy in vectors_x:
        copy.start()

    def pack(h, xx):
        @pl.loop(0, NY)
        def _(k):
            first = pl.multiple_of((xx * NY + k) * 24, 8)
            chunk = g[pl.ds(first, 24), :]
            sx[h, xx, k] = jnp.concatenate([fold(chunk[0:12]), fold(chunk[12:24])], axis=0).astype(bf16)

    left, right, far = (x + 3) % NX, (x + 1) % NX, (x + 2) % NX
    low, high = pl.ds(0, NY // 2), pl.ds(NY // 2, NY // 2)

    def along_x(h, n):
        source_ref, to = [
            (sx.at[h, far, low], left), (sx.at[h, far, high], right),
            (sx.at[h, right, low], right), (sx.at[h, left, high], left),
            (relay.at[h, 0], left), (relay.at[h, 1], right),
        ][n]
        return remote(source_ref, rx.at[h, n], sem_sx.at[h, n], sem_rx.at[h, n], at(to, y, z))

    def pass_on(h):
        for n in range(2):
            along_x(h, n).wait_recv()
            half = sx[h, left, low] if n == 0 else sx[h, right, high]
            relay[h, n] = (rx[h, n].astype(f32) + half.astype(f32)).astype(bf16)
            along_x(h, 4 + n).start()

    def along_y(h, d):
        to = (y + d) % NY
        return remote(sy.at[h, to], ry.at[h, d - 1], sem_sy.at[h, d - 1], sem_ry.at[h, d - 1], at(x, to, z))

    def along_z(h):
        return remote(sz.at[h, 1 - z], rz.at[h], sem_z.at[h, 0], sem_z.at[h, 1], at(x, y, 1 - z))

    vectors_y = [remote(vy.at[y], vy.at[y], sem_vsy.at[d - 1], sem_vry.at[d - 1], at(x, (y + d) % NY, z)) for d in range(1, NY)]
    vectors_z = remote(vz.at[0], vz.at[1], sem_vz.at[0], sem_vz.at[1], at(x, y, 1 - z))

    def piece(h, carry):
        lanes = pl.ds(pl.multiple_of(h * PIECE, PIECE), PIECE)
        g[...] = jnp.dot(
            xt[...], dlow[:, :, lanes].reshape(SLOTS * MAIN, PIECE), preferred_element_type=f32) + jnp.dot(
            xt_t[...], dlow_t[:, lanes], preferred_element_type=f32)
        pack(h, far)
        along_x(h, 0).start()
        along_x(h, 1).start()
        pack(h, right)
        along_x(h, 2).start()
        pack(h, left)
        along_x(h, 3).start()
        pack(h, x)

        @pl.when(h > 0)
        def _():
            pass_on(h - 1)
        return carry
    lax.fori_loop(0, N_PIECES, piece, 0)

    def sum_x(h):
        for n in range(2, 6):
            along_x(h, n).wait_recv()

        @pl.loop(0, NY // 2)
        def _(k):
            for n in range(2):
                own = k + n * (NY // 2)
                total = sx[h, x, own].astype(f32) + (rx[h, 2 + n, k].astype(f32) + rx[h, 4 + n, k].astype(f32))
                accx[h, own] = total
                sy[h, own] = total.astype(bf16)
        for d in range(1, NY):
            along_y(h, d).start()

    def sum_y(h):
        total = accx[h, y]
        for d in range(1, NY):
            along_y(h, d).wait_recv()
            total = total + ry[h, d - 1].astype(f32)
        sz[h, 0] = total[0:8]
        sz[h, 1] = total[8:16]
        along_z(h).start()

    for copy in vectors_x:
        copy.wait_recv()
    vy[y] = (vx[0] + vx[1]) + (vx[2] + vx[3])
    for copy in vectors_y:
        copy.start()
    pass_on(N_PIECES - 1)
    sum_x(0)
    sum_x(1)
    d_user_vec = lax.dot_general(d_score, embed, (((0,), (0,)), ((), ())), preferred_element_type=f32)
    uvec[...] = (d_user_vec * score_scale).astype(bf16)

    @pl.loop(0, D // 256)
    def _(m):
        lanes = pl.ds(pl.multiple_of(m * 256, 256), 256)
        duser_ref[:, lanes] = jnp.dot(uvec[...], proj_t[:, lanes], preferred_element_type=f32).astype(bf16)

    sum_x(2)
    for copy in vectors_y:
        copy.wait_recv()
    vz[0] = ((vy[0] + vy[1]) + (vy[2] + vy[3])) + ((vy[4] + vy[5]) + (vy[6] + vy[7]))
    vectors_z.start()
    for h in range(N_PIECES):
        sum_y(h)
    scale = 1.0 / (NX * NY * NZ)
    vectors_z.wait_recv()
    folded = (vz[0] + vz[1]) * scale
    bout_ref[...] = tile_to_row(folded[0:8])
    gout_ref[...] = tile_to_row(folded[8:16])
    for h in range(N_PIECES):
        along_z(h).wait_recv()
        rows = unfold((sz[h, z] + rz[h]) * scale)
        for r in range(ROWS_DEV):
            out_ref[r, :, h * PIECE : (h + 1) * PIECE] = rows[r : r + 1]
    for copy in started + returned + vectors_x + vectors_y + [vectors_z]:
        copy.wait_send()
    for h in range(N_PIECES):
        for n in range(6):
            along_x(h, n).wait_send()
        for d in range(1, NY):
            along_y(h, d).wait_send()
        along_z(h).wait_send()


def copy_kernel(*refs):
    n = len(refs) // 2
    copies = [pltpu.make_async_copy(refs[i], refs[n + i], refs[-1].at[i]) for i in range(n)]
    for copy in copies:
        copy.start()
    for copy in copies:
        copy.wait()


def copy_out(arrays):
    return pl.pallas_call(
        copy_kernel,
        out_shape=[jax.ShapeDtypeStruct(a.shape, a.dtype) for a in arrays],
        in_specs=[pl.BlockSpec(memory_space=pltpu.VMEM)] * len(arrays),
        out_specs=[pl.BlockSpec(memory_space=pl.ANY)] * len(arrays),
        scratch_shapes=[pltpu.SemaphoreType.DMA((len(arrays),))],
        compiler_params=pltpu.CompilerParams(vmem_limit_bytes=60 * 1024 * 1024),
        name="copy_out",
    )(*arrays)


def train_step(blocks, ids, live, positives, patches, weight, bias, gain, item_bias, users, proj):
    vmem = pl.BlockSpec(memory_space=pltpu.VMEM)
    smem = pl.BlockSpec(memory_space=pltpu.SMEM)
    anywhere = pl.BlockSpec(memory_space=pl.ANY)
    dma = pltpu.SemaphoreType.DMA
    return pl.pallas_call(
        step_kernel,
        out_shape=(
            jax.ShapeDtypeStruct((USERS_DEV, D), bf16),
            jax.ShapeDtypeStruct((ROWS_DEV, 1, D), f32),
            jax.ShapeDtypeStruct((1, D), f32),
            jax.ShapeDtypeStruct((1, D), f32),
        ),
        in_specs=[smem] * 3 + [vmem] * 2 + [anywhere] + [vmem] * 2 + [anywhere] * 3,
        out_specs=[vmem] * 4,
        scratch_shapes=[
            pltpu.VMEM((BLOCKS_DEV, MAIN, D), bf16),
            pltpu.VMEM((BLOCKS_DEV, 8, LANES), f32),
            pltpu.VMEM((N_ENC, CAP, MAIN, D), bf16),
            pltpu.VMEM((N_ENC, CAP, MAIN, D), bf16),
        ] + [pltpu.VMEM((N_ENC, 16, LANES), bf16)] * 2 + [
            pltpu.VMEM((32, D), f32),
            pltpu.VMEM((32, D), bf16),
        ] + [pltpu.VMEM((N_ENC, 16, LANES), bf16)] * 4 + [
            pltpu.VMEM((4 * MAIN, D), f32),
            pltpu.VMEM((SLOTS, MAIN, D), f32),
            pltpu.VMEM((SLOTS, MAIN, D), f32),
            pltpu.VMEM((SLOTS, MAIN, LANES), f32),
            pltpu.VMEM((32, D), f32),
            pltpu.VMEM((32, D), f32),
            pltpu.VMEM((32, D), f32),
            pltpu.VMEM((32, LANES), f32),
            pltpu.VMEM((32, D), f32),
            pltpu.VMEM((32, D), f32),
            pltpu.VMEM((SLOTS, MAIN, D), bf16),
            pltpu.VMEM((32, D), bf16),
            pltpu.VMEM((USERS_DEV, D), bf16),
            pltpu.VMEM((8, D), f32),
            pltpu.VMEM((D, PIECE), f32),
            pltpu.VMEM((D, D), bf16),
            pltpu.VMEM((512, LANES), f32),
            pltpu.VMEM((USERS_DEV, D), bf16),
            pltpu.VMEM((D, D), bf16),
            pltpu.VMEM((D, D), bf16),
            pltpu.VMEM((D, SLOTS * MAIN), bf16),
            pltpu.VMEM((D, 32), bf16),
            pltpu.VMEM((N_PIECES, NX, NY, 16, FOLD), bf16),
            pltpu.VMEM((N_PIECES, 6, NY // 2, 16, FOLD), bf16),
            pltpu.VMEM((N_PIECES, 2, NY // 2, 16, FOLD), bf16),
            pltpu.VMEM((N_PIECES, NY, 16, FOLD), bf16),
            pltpu.VMEM((N_PIECES, NY - 1, 16, FOLD), bf16),
            pltpu.VMEM((N_PIECES, NY, 16, FOLD), f32),
            pltpu.VMEM((N_PIECES, 2, 8, FOLD), f32),
            pltpu.VMEM((N_PIECES, 8, FOLD), f32),
            pltpu.VMEM((16, LANES), f32),
            pltpu.VMEM((NX, 16, LANES), f32),
            pltpu.VMEM((NY, 16, LANES), f32),
            pltpu.VMEM((2, 16, LANES), f32),
        ] + [dma((N_ENC,))] * 8 + [
            dma((N_PIECES, 6)), dma((N_PIECES, 6)), dma((N_PIECES, NY - 1)), dma((N_PIECES, NY - 1)),
            dma((N_PIECES, 2)),
            dma((NX - 1,)), dma((NX - 1,)), dma((NY - 1,)), dma((NY - 1,)), dma((2,)), dma((4,)),
        ],
        compiler_params=pltpu.CompilerParams(
            collective_id=0, has_side_effects=True, vmem_limit_bytes=56 * 1024 * 1024),
        name="train_step",
    )(blocks, ids, live, positives, patches, weight, bias, gain, item_bias, users, proj)


def body(
    patches,
    item_counts,
    item_ids,
    block_dest,
    enc_weight,
    enc_bias,
    enc_gain,
    item_bias,
    user_state,
    user_proj,
    positives,
):
    outs = train_step(
        block_dest, item_ids, item_counts, positives.reshape(-1, LANES), jnp.transpose(patches, (1, 0, 2)), enc_weight[0], enc_bias, enc_gain,
        item_bias.reshape(-1, LANES), user_state, user_proj)
    d_user, mine, d_bias, d_gain = copy_out(outs)
    return (d_user, jnp.transpose(mine, (1, 0, 2)), d_bias, d_gain)


def solution(mesh):
    return jax.shard_map(
        body,
        mesh=mesh,
        in_specs=(
            P(("dp", "enc"), None, None),
            P(("dp", "enc")),
            P(("dp", "enc")),
            P(("dp", "enc")),
            P("enc", None, None),
            P("enc", None),
            P("enc", None),
            P(),
            P(("dp", "enc"), None),
            P(),
            P(("dp", "enc")),
        ),
        out_specs=(P(("dp", "enc"), None), P("enc", "dp", None), P("enc", None), P("enc", None)),
        check_vma=False,
    )
```

```python
import jax
import jax.numpy as jnp
from jax import lax
from jax.experimental import pallas as pl
from jax.experimental.pallas import tpu as pltpu
from jax.sharding import PartitionSpec as P

D = 768
PATCHES = 196
BLOCK_ROWS = 49
BLOCKS_ITEM = 4
ITEMS_DEV = 4
BLOCKS_DEV = ITEMS_DEV * BLOCKS_ITEM
USERS_DEV = 256
CAP = 2
N_ENC = 12
SLOTS = N_ENC * CAP
MAIN = 48
NX, NY, NZ = 4, 8, 2
ROWS_DEV = 12
PIECE = 256
N_PIECES = D // PIECE
FOLD = 384
LANES = 128
PIECES = D // LANES
GROUP = 16

score_scale = 0.1
loss_weight = 16.0
norm_eps = 1e-05
GELU_A = 0.7978845608028654
GELU_B = 0.044715

f32 = jnp.float32
bf16 = jnp.bfloat16


def fold(rows):
    tail = rows[8:12]
    return jnp.concatenate([rows[0:8], jnp.concatenate([tail[:, :LANES], tail[:, LANES:]], axis=0)], axis=1)


def unfold(folded):
    tail = folded[:, PIECE:]
    return jnp.concatenate([folded[:, :PIECE], jnp.concatenate([tail[0:4], tail[4:8]], axis=1)], axis=0)


def row_to_tile(row):
    pieces = [row[:, c * LANES : (c + 1) * LANES] for c in range(PIECES)]
    return jnp.concatenate(pieces + [jnp.zeros((2, LANES), row.dtype)], axis=0)


def tile_to_row(tile):
    return jnp.concatenate([tile[c : c + 1] for c in range(PIECES)], axis=1)


def sign3(core):
    return 1 - 2 * core


def offset(p, core):
    return ((p + 1) // 2) * (2 * (p % 2) - 1) * (1 + (p // 5) * (sign3(core) - 1))


def normed_rows(projected, bias, gain):
    shifted = projected + bias
    center = jnp.sum(shifted, axis=-1, keepdims=True) * (1.0 / D)
    deviation = shifted - center
    variance = jnp.sum(deviation * deviation, axis=-1, keepdims=True) * (1.0 / D)
    rstd = lax.rsqrt(variance + norm_eps)
    xhat = deviation * rstd
    n = xhat * gain
    square = n * n
    t = jnp.tanh(n * (GELU_A + (GELU_A * GELU_B) * square))
    half = 0.5 + 0.5 * t
    act = n * half
    slope = half + (0.5 * n) * (1.0 - t * t) * (GELU_A + (3.0 * GELU_A * GELU_B) * square)
    return act, slope, xhat, rstd


def rows_back(u, slope, xhat, rstd):
    t = slope * u
    m1 = jnp.sum(t, axis=-1, keepdims=True) * (1.0 / D)
    m2 = jnp.sum(t * xhat, axis=-1, keepdims=True) * (1.0 / D)
    return rstd * (t - m1 - xhat * m2)


def step_kernel(
    blocks_ref, ids_ref, live_ref, positives_ref, patches_ref, w_hbm, bias_ref, gain_ref, ibias_hbm,
    users_hbm, proj_hbm,
    duser_ref, out_ref, bout_ref, gout_ref,
    main, tails, send, recv, tsend, trecv, trows, xtail, psend, precv, dsend, drecv,
    proj, xhat_m, slope_m, rstd_m, act_t, xhat_t, slope_t, rstd_t, dtail, gsum, dlow, dlow_t, uvec, dbacc, g,
    w_ref, ibias_ref, users_ref, proj_ref, proj_t, uvec_t, belongs_t, xt, xt_t,
    sx, rx, relay, sy, ry, accx, sz, rz, vown, vx, vy, vz,
    sem_s, sem_r, sem_ts, sem_tr, sem_ps, sem_pr, sem_ds, sem_dr,
    sem_sx, sem_rx, sem_sy, sem_ry, sem_z, sem_vsx, sem_vrx, sem_vsy, sem_vry, sem_vz, sem_load,
):
    dp = lax.axis_index("dp")
    enc = lax.axis_index("enc")
    x = dp // (NY * NZ)
    y = (dp // NZ) % NY
    z = dp % NZ
    core = enc % 2
    ring = z * 6 + enc // 2

    def at(xx, yy, zz):
        return {"dp": (xx * NY + yy) * NZ + zz}

    def on_ring(place, which):
        place = (place + 12) % 12
        return {"dp": (x * NY + y) * NZ + place // 6, "enc": (place % 6) * 2 + which}

    def dest(p, r):
        return on_ring(ring + offset(p, core), (core + r) % 2)

    def source(p, r):
        other = (core + r) % 2
        return on_ring(ring - offset(p, other), other)

    loads = [
        pltpu.make_async_copy(there, here, sem_load.at[n])
        for n, (there, here) in enumerate(
            [(users_hbm, users_ref), (proj_hbm, proj_ref), (ibias_hbm, ibias_ref), (w_hbm, w_ref)])
    ]
    barrier = pltpu.get_barrier_semaphore()
    partners = 0
    for p in range(6):
        for r in range(2):
            if p or r:
                pl.semaphore_signal(barrier, inc=1, device_id=source(p, r))
                partners += 1
    for d in range(1, NX):
        pl.semaphore_signal(barrier, inc=1, device_id=at((x + d) % NX, y, z))
    for d in range(1, NY):
        pl.semaphore_signal(barrier, inc=1, device_id=at(x, (y + d) % NY, z))
    pl.semaphore_signal(barrier, inc=1, device_id=at(x, y, 1 - z))
    partners += NX + NY - 1
    for load in loads:
        load.start()

    n_live = live_ref[0] * BLOCKS_ITEM
    named = [jnp.where(b < n_live, blocks_ref[b], -1) for b in range(BLOCKS_DEV)]
    src = []
    lane_slot = lax.broadcasted_iota(jnp.int32, (1, N_ENC * 16), 1) >> 3
    items = jnp.full((1, N_ENC * 16), -1, jnp.int32)
    for j in range(N_ENC):
        expert = dest(j // 2, j % 2)["enc"]
        low, high = jnp.int32(BLOCKS_DEV), jnp.int32(-1)
        for b in range(BLOCKS_DEV):
            high = jnp.where(named[b] == expert, b, high)
            back = BLOCKS_DEV - 1 - b
            low = jnp.where(named[back] == expert, back, low)
        src.append(jnp.minimum(low, BLOCKS_DEV - 1))
        src.append(jnp.maximum(high, 0))
        items = jnp.where(lane_slot == 2 * j, jnp.where(low < BLOCKS_DEV, low >> 2, -1), items)
        items = jnp.where(lane_slot == 2 * j + 1, jnp.where(high > low, high >> 2, -1), items)

    tails[...] = jnp.zeros_like(tails)
    row = lax.broadcasted_iota(jnp.int32, (208, PATCHES), 0)
    col = lax.broadcasted_iota(jnp.int32, (208, PATCHES), 1)
    steps = (row >= 48).astype(jnp.int32) + (row >= 96).astype(jnp.int32) + (row >= 144).astype(jnp.int32)
    origin = jnp.where(row < 192, row + steps, (row - 192) * BLOCK_ROWS + MAIN)
    order = jnp.where(origin == col, 1.0, 0.0).astype(bf16)
    for i in range(ITEMS_DEV):
        sorted_rows = jnp.dot(order, patches_ref[:, i, :], preferred_element_type=f32)
        for b in range(BLOCKS_ITEM):
            main[i * BLOCKS_ITEM + b] = sorted_rows[b * MAIN : (b + 1) * MAIN].astype(bf16)
            tails[i * BLOCKS_ITEM + b] = row_to_tile(sorted_rows[192 + b : 193 + b])

    def remote(src, dst, ssem, rsem, device):
        return pltpu.make_async_remote_copy(
            src_ref=src, dst_ref=dst, send_sem=ssem, recv_sem=rsem, device_id=device)

    def tail_tile(j):
        return jnp.concatenate([tails[src[2 * j]], tails[src[2 * j + 1]]], axis=0).astype(bf16)

    trecv[0] = tail_tile(0)
    for j in range(1, N_ENC):
        tsend[j] = tail_tile(j)
    pl.semaphore_wait(barrier, partners)
    started = []

    def start(copy):
        copy.start()
        started.append(copy)
        return copy

    for p in (5, 4, 3, 2, 1, 0):
        if p == 5:
            for j in range(1, N_ENC):
                start(remote(tsend.at[j], trecv.at[j], sem_ts.at[j], sem_tr.at[j], dest(j // 2, j % 2)))
        for r in range(2):
            j = 2 * p + r
            if j:
                for k in range(CAP):
                    send[j, k] = main[src[2 * j + k]]
                start(remote(send.at[j], recv.at[j], sem_s.at[j], sem_r.at[j], dest(p, r)))
    for k in range(CAP):
        recv[0, k] = main[src[k]]

    for load in loads:
        load.wait()

    @pl.loop(0, D // 256)
    def _(m):
        first = pl.multiple_of(m * 256, 256)
        uvec[:, pl.ds(first, 256)] = jnp.dot(
            users_ref[...], proj_ref[:, pl.ds(first, 256)], preferred_element_type=f32).astype(bf16)

    @pl.loop(0, PIECES)
    def _(c):
        lanes = pl.ds(pl.multiple_of(c * LANES, LANES), LANES)
        proj_t[lanes, :] = proj_ref[:, lanes].T

    entry = lax.broadcasted_iota(jnp.int32, (512, LANES), 0) * LANES + lax.broadcasted_iota(jnp.int32, (512, LANES), 1)
    item_row = lax.broadcasted_iota(jnp.int32, (8, 1), 0)
    item_biases = jnp.zeros((8, 1), f32)
    for i in range(ITEMS_DEV):
        picked = jnp.where(entry == ids_ref[i], ibias_ref[...], 0.0)
        picked = jnp.sum(jnp.sum(picked, axis=0, keepdims=True), axis=1, keepdims=True)
        item_biases = item_biases + jnp.where(item_row == i, picked, 0.0)

    out_row = lax.broadcasted_iota(jnp.int32, (48, N_ENC * 16), 0)
    in_col = lax.broadcasted_iota(jnp.int32, (48, N_ENC * 16), 1)
    belongs = ((out_row & 7) == items) & ((out_row >> 3) == (in_col & 7))
    belongs = jnp.where(belongs, 1.0, 0.0).astype(bf16)

    belongs_t[...] = belongs.astype(f32).T.astype(bf16)
    for c in range(PIECES):
        uvec_t[c * LANES : (c + 1) * LANES, :] = uvec[:, c * LANES : (c + 1) * LANES].T

    bias = bias_ref[...]
    gain = gain_ref[...]

    trows[...] = jnp.zeros_like(trows)
    for j in range(N_ENC):
        if j:
            remote(tsend.at[j], trecv.at[j], sem_ts.at[j], sem_tr.at[j], dest(j // 2, j % 2)).wait_recv()
        tile = trecv[j].astype(f32)
        for k in range(CAP):
            trows[2 * j + k : 2 * j + k + 1, :] = tile_to_row(tile[8 * k : 8 * k + 8])
    xtail[...] = trows[...].astype(bf16)
    xt_t[...] = trows[...].T.astype(bf16)
    proj[0:32, :] = jnp.dot(xtail[...], w_ref[...], preferred_element_type=f32)
    for s in range(2):
        rows = slice(s * GROUP, (s + 1) * GROUP)
        act, slope, xhat, rstd = normed_rows(proj[rows, :], bias, gain)
        act_t[rows, :] = act
        slope_t[rows, :] = slope
        xhat_t[rows, :] = xhat
        rstd_t[rows, :] = jnp.broadcast_to(rstd, (GROUP, LANES))

    def forward(q, carry):
        p = (6 - q) % 6
        for r in range(2):
            @pl.when(2 * p + r > 0)
            def _():
                remote(send.at[2 * p + r], recv.at[2 * p + r], sem_s.at[2 * p + r], sem_r.at[2 * p + r],
                       {"enc": (enc // 2) * 2 + 1 - core}).wait_recv()
        @pl.loop(0, D // 256)
        def _(m):
            first = pl.multiple_of(m * 256, 256)
            proj[:, pl.ds(first, 256)] = jnp.dot(
                recv[pl.ds(2 * p, 2)].reshape(4 * MAIN, D), w_ref[:, pl.ds(first, 256)], preferred_element_type=f32)

        def slot(s, carry):
            own = 4 * p + s
            pooled = act_t[pl.ds(own, 1), :]
            weighted = slope_t[pl.ds(own, 1), :] * xhat_t[pl.ds(own, 1), :]
            pool, gs = None, None
            for m in range(MAIN // GROUP):
                act, slope, xhat, rstd = normed_rows(
                    proj[pl.ds(pl.multiple_of(s * MAIN + m * GROUP, GROUP), GROUP), :], bias, gain)
                rows = slice(m * GROUP, (m + 1) * GROUP)
                slope_m[own, rows, :] = slope
                xhat_m[own, rows, :] = xhat
                rstd_m[own, rows, :] = jnp.broadcast_to(rstd, (GROUP, LANES))
                product = slope * xhat
                act = act[0:8] + act[8:16]
                product = product[0:8] + product[8:16]
                pool = act if pool is None else pool + act
                gs = product if gs is None else gs + product
            gsum[pl.ds(own, 1), :] = jnp.sum(gs, axis=0, keepdims=True) + weighted
            trows[pl.ds(own, 1), :] = jnp.sum(pool, axis=0, keepdims=True) + pooled
            return carry
        lax.fori_loop(0, 4, slot, 0, unroll=True)
        for r in range(2):
            j = 2 * p + r
            tile = jnp.concatenate(
                [row_to_tile(trows[pl.ds(2 * j + k, 1), :]) for k in range(CAP)], axis=0).astype(bf16)
            psend[j] = tile
            if r == 0:
                @pl.when(p == 0)
                def _():
                    precv[0] = tile

            @pl.when(j > 0)
            def _():
                remote(psend.at[j], precv.at[j], sem_ps.at[j], sem_pr.at[j], source(p, r)).start()
        return carry
    lax.fori_loop(0, 6, forward, 0)

    returned = [remote(psend.at[j], precv.at[j], sem_ps.at[j], sem_pr.at[j], source(j // 2, j % 2)) for j in range(1, N_ENC)]

    def turn(c, carry):
        lanes = pl.ds(pl.multiple_of(c * LANES, LANES), LANES)
        xt[lanes, :] = recv[:, :, :, lanes].reshape(SLOTS * MAIN, LANES).T
        return carry
    lax.fori_loop(0, PIECES // 2, turn, 0)
    for copy in returned:
        copy.wait_recv()
    summed = jnp.dot(belongs, precv[...].reshape(N_ENC * 16, LANES), preferred_element_type=f32)
    embed = jnp.concatenate([summed[8 * c : 8 * c + 8] for c in range(PIECES)], axis=1)
    embed = (embed / PATCHES).astype(bf16)
    scores = jnp.dot(embed, uvec_t[...], preferred_element_type=f32)
    scores = scores * score_scale + item_biases
    index = lax.broadcasted_iota(jnp.int32, (8, USERS_DEV), 0)
    chosen = positives_ref[...].astype(f32)
    chosen = jnp.concatenate([chosen[0:1], chosen[1:2]], axis=1)
    live = live_ref[0].astype(f32)
    chosen = chosen - live * jnp.floor((chosen + 0.5) / live)
    target = jnp.where(index.astype(f32) == chosen, 1.0, 0.0)
    sigmoid = 1.0 / (1.0 + jnp.exp(-scores))
    d_score = jnp.where(index < live_ref[0], loss_weight * (sigmoid - target), 0.0).astype(bf16)
    d_embed = jnp.dot(d_score, uvec[...], preferred_element_type=f32) * score_scale
    d_folded = jnp.concatenate([d_embed[:, c * LANES : (c + 1) * LANES] for c in range(PIECES)], axis=0).astype(bf16)
    d_slots = jnp.dot(belongs_t[...], d_folded, preferred_element_type=f32)
    dsend[...] = d_slots.astype(bf16).reshape(N_ENC, 16, LANES)
    for p in (5, 4, 3, 2, 1, 0):
        for r in range(2):
            j = 2 * p + r
            if j:
                start(remote(dsend.at[j], drecv.at[j], sem_ds.at[j], sem_dr.at[j], dest(p, r)))
    drecv[0] = dsend[0]
    lax.fori_loop(PIECES // 2, PIECES, turn, 0)

    dtail[...] = jnp.zeros_like(dtail)
    dbacc[...] = jnp.zeros_like(dbacc)

    def backward(j, carry):
        @pl.when(j > 0)
        def _():
            remote(dsend.at[j], drecv.at[j], sem_ds.at[j], sem_dr.at[j],
                   {"enc": (enc // 2) * 2 + 1 - core}).wait_recv()
        tile = drecv[j].astype(f32) / PATCHES
        for k in range(CAP):
            own = 2 * j + k
            d_row = tile_to_row(tile[8 * k : 8 * k + 8])
            dtail[pl.ds(own, 1), :] = d_row
            u = d_row * gain
            for m in range(MAIN // GROUP):
                rows = slice(m * GROUP, (m + 1) * GROUP)
                rstd = jnp.concatenate([rstd_m[own, rows, :]] * PIECES, axis=1)
                d_projected = rows_back(u, slope_m[own, rows, :], xhat_m[own, rows, :], rstd)
                dlow[own, rows, :] = d_projected.astype(bf16)
                dbacc[...] += d_projected[0:8] + d_projected[8:16]
        return carry
    lax.fori_loop(0, N_ENC, backward, 0)
    for s in range(2):
        rows = slice(s * GROUP, (s + 1) * GROUP)
        rstd = jnp.concatenate([rstd_t[rows, :]] * PIECES, axis=1)
        d_projected = rows_back(dtail[rows, :] * gain, slope_t[rows, :], xhat_t[rows, :], rstd)
        dlow_t[rows, :] = d_projected.astype(bf16)
        dbacc[...] += d_projected[0:8] + d_projected[8:16]
    d_bias = jnp.sum(dbacc[...], axis=0, keepdims=True)
    d_gain = jnp.sum(dtail[0:SLOTS, :] * gsum[0:SLOTS, :], axis=0, keepdims=True)
    vectors = jnp.concatenate([row_to_tile(d_bias), row_to_tile(d_gain)], axis=0)

    vown[...] = vectors
    vx[x] = vectors
    vectors_x = [remote(vown, vx.at[x], sem_vsx.at[d - 1], sem_vrx.at[d - 1], at((x + d) % NX, y, z)) for d in range(1, NX)]
    for copy in vectors_x:
        copy.start()

    def pack(h, xx):
        @pl.loop(0, NY)
        def _(k):
            first = pl.multiple_of((xx * NY + k) * 24, 8)
            chunk = g[pl.ds(first, 24), :]
            sx[h, xx, k] = jnp.concatenate([fold(chunk[0:12]), fold(chunk[12:24])], axis=0).astype(bf16)

    left, right, far = (x + 3) % NX, (x + 1) % NX, (x + 2) % NX
    low, high = pl.ds(0, NY // 2), pl.ds(NY // 2, NY // 2)

    def along_x(h, n):
        source_ref, to = [
            (sx.at[h, far, low], left), (sx.at[h, far, high], right),
            (sx.at[h, right, low], right), (sx.at[h, left, high], left),
            (relay.at[h, 0], left), (relay.at[h, 1], right),
        ][n]
        return remote(source_ref, rx.at[h, n], sem_sx.at[h, n], sem_rx.at[h, n], at(to, y, z))

    def pass_on(h):
        for n in range(2):
            along_x(h, n).wait_recv()
            half = sx[h, left, low] if n == 0 else sx[h, right, high]
            relay[h, n] = (rx[h, n].astype(f32) + half.astype(f32)).astype(bf16)
            along_x(h, 4 + n).start()

    def along_y(h, d):
        to = (y + d) % NY
        return remote(sy.at[h, to], ry.at[h, d - 1], sem_sy.at[h, d - 1], sem_ry.at[h, d - 1], at(x, to, z))

    def along_z(h):
        return remote(sz.at[h, 1 - z], rz.at[h], sem_z.at[h, 0], sem_z.at[h, 1], at(x, y, 1 - z))

    vectors_y = [remote(vy.at[y], vy.at[y], sem_vsy.at[d - 1], sem_vry.at[d - 1], at(x, (y + d) % NY, z)) for d in range(1, NY)]
    vectors_z = remote(vz.at[0], vz.at[1], sem_vz.at[0], sem_vz.at[1], at(x, y, 1 - z))

    def piece(h, carry):
        lanes = pl.ds(pl.multiple_of(h * PIECE, PIECE), PIECE)
        g[...] = jnp.dot(
            xt[...], dlow[:, :, lanes].reshape(SLOTS * MAIN, PIECE), preferred_element_type=f32) + jnp.dot(
            xt_t[...], dlow_t[:, lanes], preferred_element_type=f32)
        pack(h, far)
        along_x(h, 0).start()
        along_x(h, 1).start()
        pack(h, right)
        along_x(h, 2).start()
        pack(h, left)
        along_x(h, 3).start()
        pack(h, x)

        @pl.when(h > 0)
        def _():
            pass_on(h - 1)
        return carry
    lax.fori_loop(0, N_PIECES, piece, 0)

    def sum_x(h):
        for n in range(2, 6):
            along_x(h, n).wait_recv()

        @pl.loop(0, NY // 2)
        def _(k):
            for n in range(2):
                own = k + n * (NY // 2)
                total = sx[h, x, own].astype(f32) + (rx[h, 2 + n, k].astype(f32) + rx[h, 4 + n, k].astype(f32))
                accx[h, own] = total
                sy[h, own] = total.astype(bf16)
        for d in range(1, NY):
            along_y(h, d).start()

    def sum_y(h):
        total = accx[h, y]
        for d in range(1, NY):
            along_y(h, d).wait_recv()
            total = total + ry[h, d - 1].astype(f32)
        sz[h, 0] = total[0:8]
        sz[h, 1] = total[8:16]
        along_z(h).start()

    for copy in vectors_x:
        copy.wait_recv()
    vy[y] = (vx[0] + vx[1]) + (vx[2] + vx[3])
    for copy in vectors_y:
        copy.start()
    sum_x(0)
    pass_on(N_PIECES - 1)
    sum_x(1)
    d_user_vec = lax.dot_general(d_score, embed, (((0,), (0,)), ((), ())), preferred_element_type=f32)
    uvec[...] = (d_user_vec * score_scale).astype(bf16)

    @pl.loop(0, D // 256)
    def _(m):
        lanes = pl.ds(pl.multiple_of(m * 256, 256), 256)
        duser_ref[:, lanes] = jnp.dot(uvec[...], proj_t[:, lanes], preferred_element_type=f32).astype(bf16)

    sum_x(2)
    for copy in vectors_y:
        copy.wait_recv()
    vz[0] = ((vy[0] + vy[1]) + (vy[2] + vy[3])) + ((vy[4] + vy[5]) + (vy[6] + vy[7]))
    vectors_z.start()
    for h in range(N_PIECES):
        sum_y(h)
    scale = 1.0 / (NX * NY * NZ)
    vectors_z.wait_recv()
    folded = (vz[0] + vz[1]) * scale
    bout_ref[...] = tile_to_row(folded[0:8])
    gout_ref[...] = tile_to_row(folded[8:16])
    for h in range(N_PIECES):
        along_z(h).wait_recv()
        rows = unfold((sz[h, z] + rz[h]) * scale)
        for r in range(ROWS_DEV):
            out_ref[r, :, h * PIECE : (h + 1) * PIECE] = rows[r : r + 1]
    for copy in started + returned + vectors_x + vectors_y + [vectors_z]:
        copy.wait_send()
    for h in range(N_PIECES):
        for n in range(6):
            along_x(h, n).wait_send()
        for d in range(1, NY):
            along_y(h, d).wait_send()
        along_z(h).wait_send()


def copy_kernel(*refs):
    n = len(refs) // 2
    copies = [pltpu.make_async_copy(refs[i], refs[n + i], refs[-1].at[i]) for i in range(n)]
    for copy in copies:
        copy.start()
    for copy in copies:
        copy.wait()


def copy_out(arrays):
    return pl.pallas_call(
        copy_kernel,
        out_shape=[jax.ShapeDtypeStruct(a.shape, a.dtype) for a in arrays],
        in_specs=[pl.BlockSpec(memory_space=pltpu.VMEM)] * len(arrays),
        out_specs=[pl.BlockSpec(memory_space=pl.ANY)] * len(arrays),
        scratch_shapes=[pltpu.SemaphoreType.DMA((len(arrays),))],
        compiler_params=pltpu.CompilerParams(vmem_limit_bytes=60 * 1024 * 1024),
        name="copy_out",
    )(*arrays)


def train_step(blocks, ids, live, positives, patches, weight, bias, gain, item_bias, users, proj):
    vmem = pl.BlockSpec(memory_space=pltpu.VMEM)
    smem = pl.BlockSpec(memory_space=pltpu.SMEM)
    anywhere = pl.BlockSpec(memory_space=pl.ANY)
    dma = pltpu.SemaphoreType.DMA
    return pl.pallas_call(
        step_kernel,
        out_shape=(
            jax.ShapeDtypeStruct((USERS_DEV, D), bf16),
            jax.ShapeDtypeStruct((ROWS_DEV, 1, D), f32),
            jax.ShapeDtypeStruct((1, D), f32),
            jax.ShapeDtypeStruct((1, D), f32),
        ),
        in_specs=[smem] * 3 + [vmem] * 2 + [anywhere] + [vmem] * 2 + [anywhere] * 3,
        out_specs=[vmem] * 4,
        scratch_shapes=[
            pltpu.VMEM((BLOCKS_DEV, MAIN, D), bf16),
            pltpu.VMEM((BLOCKS_DEV, 8, LANES), f32),
            pltpu.VMEM((N_ENC, CAP, MAIN, D), bf16),
            pltpu.VMEM((N_ENC, CAP, MAIN, D), bf16),
        ] + [pltpu.VMEM((N_ENC, 16, LANES), bf16)] * 2 + [
            pltpu.VMEM((32, D), f32),
            pltpu.VMEM((32, D), bf16),
        ] + [pltpu.VMEM((N_ENC, 16, LANES), bf16)] * 4 + [
            pltpu.VMEM((4 * MAIN, D), f32),
            pltpu.VMEM((SLOTS, MAIN, D), f32),
            pltpu.VMEM((SLOTS, MAIN, D), f32),
            pltpu.VMEM((SLOTS, MAIN, LANES), f32),
            pltpu.VMEM((32, D), f32),
            pltpu.VMEM((32, D), f32),
            pltpu.VMEM((32, D), f32),
            pltpu.VMEM((32, LANES), f32),
            pltpu.VMEM((32, D), f32),
            pltpu.VMEM((32, D), f32),
            pltpu.VMEM((SLOTS, MAIN, D), bf16),
            pltpu.VMEM((32, D), bf16),
            pltpu.VMEM((USERS_DEV, D), bf16),
            pltpu.VMEM((8, D), f32),
            pltpu.VMEM((D, PIECE), f32),
            pltpu.VMEM((D, D), bf16),
            pltpu.VMEM((512, LANES), f32),
            pltpu.VMEM((USERS_DEV, D), bf16),
            pltpu.VMEM((D, D), bf16),
            pltpu.VMEM((D, D), bf16),
            pltpu.VMEM((D, USERS_DEV), bf16),
            pltpu.VMEM((N_ENC * 16, 48), bf16),
            pltpu.VMEM((D, SLOTS * MAIN), bf16),
            pltpu.VMEM((D, 32), bf16),
            pltpu.VMEM((N_PIECES, NX, NY, 16, FOLD), bf16),
            pltpu.VMEM((N_PIECES, 6, NY // 2, 16, FOLD), bf16),
            pltpu.VMEM((N_PIECES, 2, NY // 2, 16, FOLD), bf16),
            pltpu.VMEM((N_PIECES, NY, 16, FOLD), bf16),
            pltpu.VMEM((N_PIECES, NY - 1, 16, FOLD), bf16),
            pltpu.VMEM((N_PIECES, NY, 16, FOLD), f32),
            pltpu.VMEM((N_PIECES, 2, 8, FOLD), f32),
            pltpu.VMEM((N_PIECES, 8, FOLD), f32),
            pltpu.VMEM((16, LANES), f32),
            pltpu.VMEM((NX, 16, LANES), f32),
            pltpu.VMEM((NY, 16, LANES), f32),
            pltpu.VMEM((2, 16, LANES), f32),
        ] + [dma((N_ENC,))] * 8 + [
            dma((N_PIECES, 6)), dma((N_PIECES, 6)), dma((N_PIECES, NY - 1)), dma((N_PIECES, NY - 1)),
            dma((N_PIECES, 2)),
            dma((NX - 1,)), dma((NX - 1,)), dma((NY - 1,)), dma((NY - 1,)), dma((2,)), dma((4,)),
        ],
        compiler_params=pltpu.CompilerParams(
            collective_id=0, has_side_effects=True, vmem_limit_bytes=56 * 1024 * 1024),
        name="train_step",
    )(blocks, ids, live, positives, patches, weight, bias, gain, item_bias, users, proj)


def body(
    patches,
    item_counts,
    item_ids,
    block_dest,
    enc_weight,
    enc_bias,
    enc_gain,
    item_bias,
    user_state,
    user_proj,
    positives,
):
    outs = train_step(
        block_dest, item_ids, item_counts, positives.reshape(-1, LANES), jnp.transpose(patches, (1, 0, 2)), enc_weight[0], enc_bias, enc_gain,
        item_bias.reshape(-1, LANES), user_state, user_proj)
    d_user, mine, d_bias, d_gain = copy_out(outs)
    return (d_user, jnp.transpose(mine, (1, 0, 2)), d_bias, d_gain)


def solution(mesh):
    return jax.shard_map(
        body,
        mesh=mesh,
        in_specs=(
            P(("dp", "enc"), None, None),
            P(("dp", "enc")),
            P(("dp", "enc")),
            P(("dp", "enc")),
            P("enc", None, None),
            P("enc", None),
            P("enc", None),
            P(),
            P(("dp", "enc"), None),
            P(),
            P(("dp", "enc")),
        ),
        out_specs=(P(("dp", "enc"), None), P("enc", "dp", None), P("enc", None), P("enc", None)),
        check_vma=False,
    )
```

```python
import jax
import jax.numpy as jnp
from jax import lax
from jax.experimental import pallas as pl
from jax.experimental.pallas import tpu as pltpu
from jax.sharding import PartitionSpec as P

D = 768
PATCHES = 196
BLOCK_ROWS = 49
BLOCKS_ITEM = 4
ITEMS_DEV = 4
BLOCKS_DEV = ITEMS_DEV * BLOCKS_ITEM
USERS_DEV = 256
CAP = 2
N_ENC = 12
SLOTS = N_ENC * CAP
MAIN = 48
NX, NY, NZ = 4, 8, 2
ROWS_DEV = 12
PIECE = 256
N_PIECES = D // PIECE
FOLD = 384
LANES = 128
PIECES = D // LANES
GROUP = 16

score_scale = 0.1
loss_weight = 16.0
norm_eps = 1e-05
GELU_A = 0.7978845608028654
GELU_B = 0.044715

f32 = jnp.float32
bf16 = jnp.bfloat16


def fold(rows):
    tail = rows[8:12]
    return jnp.concatenate([rows[0:8], jnp.concatenate([tail[:, :LANES], tail[:, LANES:]], axis=0)], axis=1)


def unfold(folded):
    tail = folded[:, PIECE:]
    return jnp.concatenate([folded[:, :PIECE], jnp.concatenate([tail[0:4], tail[4:8]], axis=1)], axis=0)


def row_to_tile(row):
    pieces = [row[:, c * LANES : (c + 1) * LANES] for c in range(PIECES)]
    return jnp.concatenate(pieces + [jnp.zeros((2, LANES), row.dtype)], axis=0)


def tile_to_row(tile):
    return jnp.concatenate([tile[c : c + 1] for c in range(PIECES)], axis=1)


def sign3(core):
    return 1 - 2 * core


def offset(p, core):
    return ((p + 1) // 2) * (2 * (p % 2) - 1) * (1 + (p // 5) * (sign3(core) - 1))


def normed_rows(projected, bias, gain):
    shifted = projected + bias
    center = jnp.sum(shifted, axis=-1, keepdims=True) * (1.0 / D)
    deviation = shifted - center
    variance = jnp.sum(deviation * deviation, axis=-1, keepdims=True) * (1.0 / D)
    rstd = lax.rsqrt(variance + norm_eps)
    xhat = deviation * rstd
    n = xhat * gain
    square = n * n
    t = jnp.tanh(n * (GELU_A + (GELU_A * GELU_B) * square))
    half = 0.5 + 0.5 * t
    act = n * half
    slope = half + (0.5 * n) * (1.0 - t * t) * (GELU_A + (3.0 * GELU_A * GELU_B) * square)
    return act, slope, xhat, rstd


def rows_back(u, slope, xhat, rstd):
    t = slope * u
    m1 = jnp.sum(t, axis=-1, keepdims=True) * (1.0 / D)
    m2 = jnp.sum(t * xhat, axis=-1, keepdims=True) * (1.0 / D)
    return rstd * (t - m1 - xhat * m2)


def step_kernel(
    blocks_ref, ids_ref, live_ref, positives_ref, patches_ref, w_hbm, bias_ref, gain_ref, ibias_hbm,
    users_hbm, proj_hbm,
    duser_ref, out_ref, bout_ref, gout_ref,
    main, tails, send, recv, tsend, trecv, trows, xtail, psend, precv, dsend, drecv,
    proj, xhat_m, slope_m, rstd_m, act_t, xhat_t, slope_t, rstd_t, dtail, gsum, dlow, dlow_t, uvec, dbacc, g,
    w_ref, ibias_ref, users_ref, proj_ref, proj_t, uvec_t, belongs_t, xt, xt_t,
    sx, rx, relay, sy, ry, accx, sz, rz, vown, vx, vy, vz,
    sem_s, sem_r, sem_ts, sem_tr, sem_ps, sem_pr, sem_ds, sem_dr,
    sem_sx, sem_rx, sem_sy, sem_ry, sem_z, sem_vsx, sem_vrx, sem_vsy, sem_vry, sem_vz, sem_load,
):
    dp = lax.axis_index("dp")
    enc = lax.axis_index("enc")
    x = dp // (NY * NZ)
    y = (dp // NZ) % NY
    z = dp % NZ
    core = enc % 2
    ring = z * 6 + enc // 2

    def at(xx, yy, zz):
        return {"dp": (xx * NY + yy) * NZ + zz}

    def on_ring(place, which):
        place = (place + 12) % 12
        return {"dp": (x * NY + y) * NZ + place // 6, "enc": (place % 6) * 2 + which}

    def dest(p, r):
        return on_ring(ring + offset(p, core), (core + r) % 2)

    def source(p, r):
        other = (core + r) % 2
        return on_ring(ring - offset(p, other), other)

    loads = [
        pltpu.make_async_copy(there, here, sem_load.at[n])
        for n, (there, here) in enumerate(
            [(users_hbm, users_ref), (proj_hbm, proj_ref), (ibias_hbm, ibias_ref), (w_hbm, w_ref)])
    ]
    barrier = pltpu.get_barrier_semaphore()
    partners = 0
    for p in range(6):
        for r in range(2):
            if p or r:
                pl.semaphore_signal(barrier, inc=1, device_id=source(p, r))
                partners += 1
    for d in range(1, NX):
        pl.semaphore_signal(barrier, inc=1, device_id=at((x + d) % NX, y, z))
    for d in range(1, NY):
        pl.semaphore_signal(barrier, inc=1, device_id=at(x, (y + d) % NY, z))
    pl.semaphore_signal(barrier, inc=1, device_id=at(x, y, 1 - z))
    partners += NX + NY - 1
    for load in loads:
        load.start()

    n_live = live_ref[0] * BLOCKS_ITEM
    named = [jnp.where(b < n_live, blocks_ref[b], -1) for b in range(BLOCKS_DEV)]
    src = []
    lane_slot = lax.broadcasted_iota(jnp.int32, (1, N_ENC * 16), 1) >> 3
    items = jnp.full((1, N_ENC * 16), -1, jnp.int32)
    for j in range(N_ENC):
        expert = dest(j // 2, j % 2)["enc"]
        low, high = jnp.int32(BLOCKS_DEV), jnp.int32(-1)
        for b in range(BLOCKS_DEV):
            high = jnp.where(named[b] == expert, b, high)
            back = BLOCKS_DEV - 1 - b
            low = jnp.where(named[back] == expert, back, low)
        src.append(jnp.minimum(low, BLOCKS_DEV - 1))
        src.append(jnp.maximum(high, 0))
        items = jnp.where(lane_slot == 2 * j, jnp.where(low < BLOCKS_DEV, low >> 2, -1), items)
        items = jnp.where(lane_slot == 2 * j + 1, jnp.where(high > low, high >> 2, -1), items)

    tails[...] = jnp.zeros_like(tails)
    row = lax.broadcasted_iota(jnp.int32, (208, PATCHES), 0)
    col = lax.broadcasted_iota(jnp.int32, (208, PATCHES), 1)
    steps = (row >= 48).astype(jnp.int32) + (row >= 96).astype(jnp.int32) + (row >= 144).astype(jnp.int32)
    origin = jnp.where(row < 192, row + steps, (row - 192) * BLOCK_ROWS + MAIN)
    order = jnp.where(origin == col, 1.0, 0.0).astype(bf16)
    for i in range(ITEMS_DEV):
        sorted_rows = jnp.dot(order, patches_ref[:, i, :], preferred_element_type=f32)
        for b in range(BLOCKS_ITEM):
            main[i * BLOCKS_ITEM + b] = sorted_rows[b * MAIN : (b + 1) * MAIN].astype(bf16)
            tails[i * BLOCKS_ITEM + b] = row_to_tile(sorted_rows[192 + b : 193 + b])

    def remote(src, dst, ssem, rsem, device):
        return pltpu.make_async_remote_copy(
            src_ref=src, dst_ref=dst, send_sem=ssem, recv_sem=rsem, device_id=device)

    def tail_tile(j):
        return jnp.concatenate([tails[src[2 * j]], tails[src[2 * j + 1]]], axis=0).astype(bf16)

    trecv[0] = tail_tile(0)
    for j in range(1, N_ENC):
        tsend[j] = tail_tile(j)
    pl.semaphore_wait(barrier, partners)
    started = []

    def start(copy):
        copy.start()
        started.append(copy)
        return copy

    for p in (5, 4, 3, 2, 1, 0):
        if p == 5:
            for j in range(1, N_ENC):
                start(remote(tsend.at[j], trecv.at[j], sem_ts.at[j], sem_tr.at[j], dest(j // 2, j % 2)))
        for r in range(2):
            j = 2 * p + r
            if j:
                for k in range(CAP):
                    send[j, k] = main[src[2 * j + k]]
                start(remote(send.at[j], recv.at[j], sem_s.at[j], sem_r.at[j], dest(p, r)))
    for k in range(CAP):
        recv[0, k] = main[src[k]]

    for load in loads:
        load.wait()

    @pl.loop(0, D // 256)
    def _(m):
        first = pl.multiple_of(m * 256, 256)
        uvec[:, pl.ds(first, 256)] = jnp.dot(
            users_ref[...], proj_ref[:, pl.ds(first, 256)], preferred_element_type=f32).astype(bf16)

    @pl.loop(0, PIECES)
    def _(c):
        lanes = pl.ds(pl.multiple_of(c * LANES, LANES), LANES)
        proj_t[lanes, :] = proj_ref[:, lanes].T

    entry = lax.broadcasted_iota(jnp.int32, (512, LANES), 0) * LANES + lax.broadcasted_iota(jnp.int32, (512, LANES), 1)
    item_row = lax.broadcasted_iota(jnp.int32, (8, 1), 0)
    item_biases = jnp.zeros((8, 1), f32)
    for i in range(ITEMS_DEV):
        picked = jnp.where(entry == ids_ref[i], ibias_ref[...], 0.0)
        picked = jnp.sum(jnp.sum(picked, axis=0, keepdims=True), axis=1, keepdims=True)
        item_biases = item_biases + jnp.where(item_row == i, picked, 0.0)

    out_row = lax.broadcasted_iota(jnp.int32, (48, N_ENC * 16), 0)
    in_col = lax.broadcasted_iota(jnp.int32, (48, N_ENC * 16), 1)
    belongs = ((out_row & 7) == items) & ((out_row >> 3) == (in_col & 7))
    belongs = jnp.where(belongs, 1.0, 0.0).astype(bf16)

    belongs_t[...] = belongs.astype(f32).T.astype(bf16)
    for c in range(PIECES):
        uvec_t[c * LANES : (c + 1) * LANES, :] = uvec[:, c * LANES : (c + 1) * LANES].T

    bias = bias_ref[...]
    gain = gain_ref[...]

    trows[...] = jnp.zeros_like(trows)
    for j in range(N_ENC):
        if j:
            remote(tsend.at[j], trecv.at[j], sem_ts.at[j], sem_tr.at[j], dest(j // 2, j % 2)).wait_recv()
        tile = trecv[j].astype(f32)
        for k in range(CAP):
            trows[2 * j + k : 2 * j + k + 1, :] = tile_to_row(tile[8 * k : 8 * k + 8])
    xtail[...] = trows[...].astype(bf16)
    xt_t[...] = trows[...].T.astype(bf16)
    proj[0:32, :] = jnp.dot(xtail[...], w_ref[...], preferred_element_type=f32)
    for s in range(2):
        rows = slice(s * GROUP, (s + 1) * GROUP)
        act, slope, xhat, rstd = normed_rows(proj[rows, :], bias, gain)
        act_t[rows, :] = act
        slope_t[rows, :] = slope
        xhat_t[rows, :] = xhat
        rstd_t[rows, :] = jnp.broadcast_to(rstd, (GROUP, LANES))

    def forward(q, carry):
        p = (6 - q) % 6
        for r in range(2):
            @pl.when(2 * p + r > 0)
            def _():
                remote(send.at[2 * p + r], recv.at[2 * p + r], sem_s.at[2 * p + r], sem_r.at[2 * p + r],
                       {"enc": (enc // 2) * 2 + 1 - core}).wait_recv()
        @pl.loop(0, D // 256)
        def _(m):
            first = pl.multiple_of(m * 256, 256)
            proj[:, pl.ds(first, 256)] = jnp.dot(
                recv[pl.ds(2 * p, 2)].reshape(4 * MAIN, D), w_ref[:, pl.ds(first, 256)], preferred_element_type=f32)

        def slot(s, carry):
            own = 4 * p + s
            pooled = act_t[pl.ds(own, 1), :]
            weighted = slope_t[pl.ds(own, 1), :] * xhat_t[pl.ds(own, 1), :]
            pool, gs = None, None
            for m in range(MAIN // GROUP):
                act, slope, xhat, rstd = normed_rows(
                    proj[pl.ds(pl.multiple_of(s * MAIN + m * GROUP, GROUP), GROUP), :], bias, gain)
                rows = slice(m * GROUP, (m + 1) * GROUP)
                slope_m[own, rows, :] = slope
                xhat_m[own, rows, :] = xhat
                rstd_m[own, rows, :] = jnp.broadcast_to(rstd, (GROUP, LANES))
                product = slope * xhat
                act = act[0:8] + act[8:16]
                product = product[0:8] + product[8:16]
                pool = act if pool is None else pool + act
                gs = product if gs is None else gs + product
            gsum[pl.ds(own, 1), :] = jnp.sum(gs, axis=0, keepdims=True) + weighted
            trows[pl.ds(own, 1), :] = jnp.sum(pool, axis=0, keepdims=True) + pooled
            return carry
        lax.fori_loop(0, 4, slot, 0, unroll=True)
        for r in range(2):
            j = 2 * p + r
            tile = jnp.concatenate(
                [row_to_tile(trows[pl.ds(2 * j + k, 1), :]) for k in range(CAP)], axis=0).astype(bf16)
            psend[j] = tile
            if r == 0:
                @pl.when(p == 0)
                def _():
                    precv[0] = tile

            @pl.when(j > 0)
            def _():
                remote(psend.at[j], precv.at[j], sem_ps.at[j], sem_pr.at[j], source(p, r)).start()
        return carry
    lax.fori_loop(0, 6, forward, 0)

    returned = [remote(psend.at[j], precv.at[j], sem_ps.at[j], sem_pr.at[j], source(j // 2, j % 2)) for j in range(1, N_ENC)]

    def turn(c, carry):
        lanes = pl.ds(pl.multiple_of(c * LANES, LANES), LANES)
        xt[lanes, :] = recv[:, :, :, lanes].reshape(SLOTS * MAIN, LANES).T
        return carry
    lax.fori_loop(0, PIECES // 2, turn, 0)
    for copy in returned:
        copy.wait_recv()
    summed = jnp.dot(belongs, precv[...].reshape(N_ENC * 16, LANES), preferred_element_type=f32)
    embed = jnp.concatenate([summed[8 * c : 8 * c + 8] for c in range(PIECES)], axis=1)
    embed = (embed / PATCHES).astype(bf16)
    scores = jnp.dot(embed, uvec_t[...], preferred_element_type=f32)
    scores = scores * score_scale + item_biases
    index = lax.broadcasted_iota(jnp.int32, (8, USERS_DEV), 0)
    chosen = positives_ref[...].astype(f32)
    chosen = jnp.concatenate([chosen[0:1], chosen[1:2]], axis=1)
    live = live_ref[0].astype(f32)
    chosen = chosen - live * jnp.floor((chosen + 0.5) / live)
    target = jnp.where(index.astype(f32) == chosen, 1.0, 0.0)
    sigmoid = 1.0 / (1.0 + jnp.exp(-scores))
    d_score = jnp.where(index < live_ref[0], loss_weight * (sigmoid - target), 0.0).astype(bf16)
    d_embed = jnp.dot(d_score, uvec[...], preferred_element_type=f32) * score_scale
    d_folded = jnp.concatenate([d_embed[:, c * LANES : (c + 1) * LANES] for c in range(PIECES)], axis=0).astype(bf16)
    d_slots = jnp.dot(belongs_t[...], d_folded, preferred_element_type=f32)
    dsend[...] = d_slots.astype(bf16).reshape(N_ENC, 16, LANES)
    for p in (5, 4, 3, 2, 1, 0):
        for r in range(2):
            j = 2 * p + r
            if j:
                start(remote(dsend.at[j], drecv.at[j], sem_ds.at[j], sem_dr.at[j], dest(p, r)))
    drecv[0] = dsend[0]
    lax.fori_loop(PIECES // 2, PIECES, turn, 0)

    dtail[...] = jnp.zeros_like(dtail)
    dbacc[...] = jnp.zeros_like(dbacc)

    def backward(j, done):
        carry = None
        @pl.when(j > 0)
        def _():
            remote(dsend.at[j], drecv.at[j], sem_ds.at[j], sem_dr.at[j],
                   {"enc": (enc // 2) * 2 + 1 - core}).wait_recv()
        tile = drecv[j].astype(f32) / PATCHES
        for k in range(CAP):
            own = 2 * j + k
            d_row = tile_to_row(tile[8 * k : 8 * k + 8])
            dtail[pl.ds(own, 1), :] = d_row
            u = d_row * gain
            for m in range(MAIN // GROUP):
                rows = slice(m * GROUP, (m + 1) * GROUP)
                rstd = jnp.concatenate([rstd_m[own, rows, :]] * PIECES, axis=1)
                d_projected = rows_back(u, slope_m[own, rows, :], xhat_m[own, rows, :], rstd)
                dlow[own, rows, :] = d_projected.astype(bf16)
                part = d_projected[0:8] + d_projected[8:16]
                carry = part if carry is None else carry + part
        dbacc[...] += carry
        return done
    lax.fori_loop(0, N_ENC, backward, 0, unroll=2)
    for s in range(2):
        rows = slice(s * GROUP, (s + 1) * GROUP)
        rstd = jnp.concatenate([rstd_t[rows, :]] * PIECES, axis=1)
        d_projected = rows_back(dtail[rows, :] * gain, slope_t[rows, :], xhat_t[rows, :], rstd)
        dlow_t[rows, :] = d_projected.astype(bf16)
        dbacc[...] += d_projected[0:8] + d_projected[8:16]
    d_bias = jnp.sum(dbacc[...], axis=0, keepdims=True)
    d_gain = jnp.sum(dtail[0:SLOTS, :] * gsum[0:SLOTS, :], axis=0, keepdims=True)
    vectors = jnp.concatenate([row_to_tile(d_bias), row_to_tile(d_gain)], axis=0)

    vown[...] = vectors
    vx[x] = vectors
    vectors_x = [remote(vown, vx.at[x], sem_vsx.at[d - 1], sem_vrx.at[d - 1], at((x + d) % NX, y, z)) for d in range(1, NX)]
    for copy in vectors_x:
        copy.start()

    def pack(h, xx):
        @pl.loop(0, NY)
        def _(k):
            first = pl.multiple_of((xx * NY + k) * 24, 8)
            chunk = g[pl.ds(first, 24), :]
            sx[h, xx, k] = jnp.concatenate([fold(chunk[0:12]), fold(chunk[12:24])], axis=0).astype(bf16)

    left, right, far = (x + 3) % NX, (x + 1) % NX, (x + 2) % NX
    low, high = pl.ds(0, NY // 2), pl.ds(NY // 2, NY // 2)

    def along_x(h, n):
        source_ref, to = [
            (sx.at[h, far, low], left), (sx.at[h, far, high], right),
            (sx.at[h, right, low], right), (sx.at[h, left, high], left),
            (relay.at[h, 0], left), (relay.at[h, 1], right),
        ][n]
        return remote(source_ref, rx.at[h, n], sem_sx.at[h, n], sem_rx.at[h, n], at(to, y, z))

    def pass_on(h):
        for n in range(2):
            along_x(h, n).wait_recv()
            half = sx[h, left, low] if n == 0 else sx[h, right, high]
            relay[h, n] = (rx[h, n].astype(f32) + half.astype(f32)).astype(bf16)
            along_x(h, 4 + n).start()

    def along_y(h, d):
        to = (y + d) % NY
        return remote(sy.at[h, to], ry.at[h, d - 1], sem_sy.at[h, d - 1], sem_ry.at[h, d - 1], at(x, to, z))

    def along_z(h):
        return remote(sz.at[h, 1 - z], rz.at[h], sem_z.at[h, 0], sem_z.at[h, 1], at(x, y, 1 - z))

    vectors_y = [remote(vy.at[y], vy.at[y], sem_vsy.at[d - 1], sem_vry.at[d - 1], at(x, (y + d) % NY, z)) for d in range(1, NY)]
    vectors_z = remote(vz.at[0], vz.at[1], sem_vz.at[0], sem_vz.at[1], at(x, y, 1 - z))

    def piece(h, carry):
        lanes = pl.ds(pl.multiple_of(h * PIECE, PIECE), PIECE)
        g[...] = jnp.dot(
            xt[...], dlow[:, :, lanes].reshape(SLOTS * MAIN, PIECE), preferred_element_type=f32) + jnp.dot(
            xt_t[...], dlow_t[:, lanes], preferred_element_type=f32)
        pack(h, far)
        along_x(h, 0).start()
        along_x(h, 1).start()
        pack(h, right)
        along_x(h, 2).start()
        pack(h, left)
        along_x(h, 3).start()
        pack(h, x)

        @pl.when(h > 0)
        def _():
            pass_on(h - 1)
        return carry
    lax.fori_loop(0, N_PIECES, piece, 0)

    def sum_x(h):
        for n in range(2, 6):
            along_x(h, n).wait_recv()

        @pl.loop(0, NY // 2)
        def _(k):
            for n in range(2):
                own = k + n * (NY // 2)
                total = sx[h, x, own].astype(f32) + (rx[h, 2 + n, k].astype(f32) + rx[h, 4 + n, k].astype(f32))
                accx[h, own] = total
                sy[h, own] = total.astype(bf16)
        for d in (4, 3, 5, 2, 6, 1, 7):
            along_y(h, d).start()

    def sum_y(h):
        total = accx[h, y]
        for d in range(1, NY):
            along_y(h, d).wait_recv()
            total = total + ry[h, d - 1].astype(f32)
        sz[h, 0] = total[0:8]
        sz[h, 1] = total[8:16]
        along_z(h).start()

    for copy in vectors_x:
        copy.wait_recv()
    vy[y] = (vx[0] + vx[1]) + (vx[2] + vx[3])
    for copy in vectors_y:
        copy.start()
    sum_x(0)
    pass_on(N_PIECES - 1)
    sum_x(1)
    sum_x(2)
    for copy in vectors_y:
        copy.wait_recv()
    vz[0] = ((vy[0] + vy[1]) + (vy[2] + vy[3])) + ((vy[4] + vy[5]) + (vy[6] + vy[7]))
    vectors_z.start()
    d_user_vec = lax.dot_general(d_score, embed, (((0,), (0,)), ((), ())), preferred_element_type=f32)
    uvec[...] = (d_user_vec * score_scale).astype(bf16)

    @pl.loop(0, D // 256)
    def _(m):
        lanes = pl.ds(pl.multiple_of(m * 256, 256), 256)
        duser_ref[:, lanes] = jnp.dot(uvec[...], proj_t[:, lanes], preferred_element_type=f32).astype(bf16)

    for h in range(N_PIECES):
        sum_y(h)
    scale = 1.0 / (NX * NY * NZ)
    vectors_z.wait_recv()
    folded = (vz[0] + vz[1]) * scale
    bout_ref[...] = tile_to_row(folded[0:8])
    gout_ref[...] = tile_to_row(folded[8:16])
    for h in range(N_PIECES):
        along_z(h).wait_recv()
        rows = unfold((sz[h, z] + rz[h]) * scale)
        for r in range(ROWS_DEV):
            out_ref[r, :, h * PIECE : (h + 1) * PIECE] = rows[r : r + 1]
    for copy in started + returned + vectors_x + vectors_y + [vectors_z]:
        copy.wait_send()
    for h in range(N_PIECES):
        for n in range(6):
            along_x(h, n).wait_send()
        for d in range(1, NY):
            along_y(h, d).wait_send()
        along_z(h).wait_send()


def copy_kernel(*refs):
    n = len(refs) // 2
    copies = [pltpu.make_async_copy(refs[i], refs[n + i], refs[-1].at[i]) for i in range(n)]
    for copy in copies:
        copy.start()
    for copy in copies:
        copy.wait()


def copy_out(arrays):
    return pl.pallas_call(
        copy_kernel,
        out_shape=[jax.ShapeDtypeStruct(a.shape, a.dtype) for a in arrays],
        in_specs=[pl.BlockSpec(memory_space=pltpu.VMEM)] * len(arrays),
        out_specs=[pl.BlockSpec(memory_space=pl.ANY)] * len(arrays),
        scratch_shapes=[pltpu.SemaphoreType.DMA((len(arrays),))],
        compiler_params=pltpu.CompilerParams(vmem_limit_bytes=2 * 1024 * 1024),
        name="copy_out",
    )(*arrays)


def train_step(blocks, ids, live, positives, patches, weight, bias, gain, item_bias, users, proj):
    vmem = pl.BlockSpec(memory_space=pltpu.VMEM)
    smem = pl.BlockSpec(memory_space=pltpu.SMEM)
    anywhere = pl.BlockSpec(memory_space=pl.ANY)
    dma = pltpu.SemaphoreType.DMA
    return pl.pallas_call(
        step_kernel,
        out_shape=(
            pltpu.VMEM((USERS_DEV, D), bf16),
            pltpu.VMEM((ROWS_DEV, 1, D), f32),
            pltpu.VMEM((1, D), f32),
            pltpu.VMEM((1, D), f32),
        ),
        in_specs=[smem] * 3 + [vmem] * 2 + [anywhere] + [vmem] * 2 + [anywhere] * 3,
        out_specs=[vmem] * 4,
        scratch_shapes=[
            pltpu.VMEM((BLOCKS_DEV, MAIN, D), bf16),
            pltpu.VMEM((BLOCKS_DEV, 8, LANES), f32),
            pltpu.VMEM((N_ENC, CAP, MAIN, D), bf16),
            pltpu.VMEM((N_ENC, CAP, MAIN, D), bf16),
        ] + [pltpu.VMEM((N_ENC, 16, LANES), bf16)] * 2 + [
            pltpu.VMEM((32, D), f32),
            pltpu.VMEM((32, D), bf16),
        ] + [pltpu.VMEM((N_ENC, 16, LANES), bf16)] * 4 + [
            pltpu.VMEM((4 * MAIN, D), f32),
            pltpu.VMEM((SLOTS, MAIN, D), f32),
            pltpu.VMEM((SLOTS, MAIN, D), f32),
            pltpu.VMEM((SLOTS, MAIN, LANES), f32),
            pltpu.VMEM((32, D), f32),
            pltpu.VMEM((32, D), f32),
            pltpu.VMEM((32, D), f32),
            pltpu.VMEM((32, LANES), f32),
            pltpu.VMEM((32, D), f32),
            pltpu.VMEM((32, D), f32),
            pltpu.VMEM((SLOTS, MAIN, D), bf16),
            pltpu.VMEM((32, D), bf16),
            pltpu.VMEM((USERS_DEV, D), bf16),
            pltpu.VMEM((8, D), f32),
            pltpu.VMEM((D, PIECE), f32),
            pltpu.VMEM((D, D), bf16),
            pltpu.VMEM((512, LANES), f32),
            pltpu.VMEM((USERS_DEV, D), bf16),
            pltpu.VMEM((D, D), bf16),
            pltpu.VMEM((D, D), bf16),
            pltpu.VMEM((D, USERS_DEV), bf16),
            pltpu.VMEM((N_ENC * 16, 48), bf16),
            pltpu.VMEM((D, SLOTS * MAIN), bf16),
            pltpu.VMEM((D, 32), bf16),
            pltpu.VMEM((N_PIECES, NX, NY, 16, FOLD), bf16),
            pltpu.VMEM((N_PIECES, 6, NY // 2, 16, FOLD), bf16),
            pltpu.VMEM((N_PIECES, 2, NY // 2, 16, FOLD), bf16),
            pltpu.VMEM((N_PIECES, NY, 16, FOLD), bf16),
            pltpu.VMEM((N_PIECES, NY - 1, 16, FOLD), bf16),
            pltpu.VMEM((N_PIECES, NY, 16, FOLD), f32),
            pltpu.VMEM((N_PIECES, 2, 8, FOLD), f32),
            pltpu.VMEM((N_PIECES, 8, FOLD), f32),
            pltpu.VMEM((16, LANES), f32),
            pltpu.VMEM((NX, 16, LANES), f32),
            pltpu.VMEM((NY, 16, LANES), f32),
            pltpu.VMEM((2, 16, LANES), f32),
        ] + [dma((N_ENC,))] * 8 + [
            dma((N_PIECES, 6)), dma((N_PIECES, 6)), dma((N_PIECES, NY - 1)), dma((N_PIECES, NY - 1)),
            dma((N_PIECES, 2)),
            dma((NX - 1,)), dma((NX - 1,)), dma((NY - 1,)), dma((NY - 1,)), dma((2,)), dma((4,)),
        ],
        compiler_params=pltpu.CompilerParams(
            collective_id=0, has_side_effects=True, vmem_limit_bytes=56 * 1024 * 1024),
        name="train_step",
    )(blocks, ids, live, positives, patches, weight, bias, gain, item_bias, users, proj)


def body(
    patches,
    item_counts,
    item_ids,
    block_dest,
    enc_weight,
    enc_bias,
    enc_gain,
    item_bias,
    user_state,
    user_proj,
    positives,
):
    outs = train_step(
        block_dest, item_ids, item_counts, positives.reshape(-1, LANES), jnp.transpose(patches, (1, 0, 2)), enc_weight[0], enc_bias, enc_gain,
        item_bias.reshape(-1, LANES), user_state, user_proj)
    d_user, mine, d_bias, d_gain = copy_out(outs)
    return (d_user, jnp.transpose(mine, (1, 0, 2)), d_bias, d_gain)


def solution(mesh):
    return jax.shard_map(
        body,
        mesh=mesh,
        in_specs=(
            P(("dp", "enc"), None, None),
            P(("dp", "enc")),
            P(("dp", "enc")),
            P(("dp", "enc")),
            P("enc", None, None),
            P("enc", None),
            P("enc", None),
            P(),
            P(("dp", "enc"), None),
            P(),
            P(("dp", "enc")),
        ),
        out_specs=(P(("dp", "enc"), None), P("enc", "dp", None), P("enc", None), P("enc", None)),
        check_vma=False,
    )
```

```python
import jax
import jax.numpy as jnp
from jax import lax
from jax.experimental import pallas as pl
from jax.experimental.pallas import tpu as pltpu
from jax.sharding import PartitionSpec as P

D = 768
PATCHES = 196
BLOCK_ROWS = 49
BLOCKS_ITEM = 4
ITEMS_DEV = 4
BLOCKS_DEV = ITEMS_DEV * BLOCKS_ITEM
USERS_DEV = 256
CAP = 2
N_ENC = 12
SLOTS = N_ENC * CAP
MAIN = 48
NX, NY, NZ = 4, 8, 2
ROWS_DEV = 12
PIECE = 256
N_PIECES = D // PIECE
FOLD = 384
LANES = 128
PIECES = D // LANES
GROUP = 16

score_scale = 0.1
loss_weight = 16.0
norm_eps = 1e-05
GELU_A = 0.7978845608028654
GELU_B = 0.044715

f32 = jnp.float32
bf16 = jnp.bfloat16


def fold(rows):
    tail = rows[8:12]
    return jnp.concatenate([rows[0:8], jnp.concatenate([tail[:, :LANES], tail[:, LANES:]], axis=0)], axis=1)


def unfold(folded):
    tail = folded[:, PIECE:]
    return jnp.concatenate([folded[:, :PIECE], jnp.concatenate([tail[0:4], tail[4:8]], axis=1)], axis=0)


def row_to_tile(row):
    pieces = [row[:, c * LANES : (c + 1) * LANES] for c in range(PIECES)]
    return jnp.concatenate(pieces + [jnp.zeros((2, LANES), row.dtype)], axis=0)


def tile_to_row(tile):
    return jnp.concatenate([tile[c : c + 1] for c in range(PIECES)], axis=1)


def sign3(core):
    return 1 - 2 * core


def offset(p, core):
    return ((p + 1) // 2) * (2 * (p % 2) - 1) * (1 + (p // 5) * (sign3(core) - 1))


def normed_rows(projected, bias, gain):
    shifted = projected + bias
    center = jnp.sum(shifted, axis=-1, keepdims=True) * (1.0 / D)
    deviation = shifted - center
    variance = jnp.sum(deviation * deviation, axis=-1, keepdims=True) * (1.0 / D)
    rstd = lax.rsqrt(variance + norm_eps)
    xhat = deviation * rstd
    n = xhat * gain
    square = n * n
    t = jnp.tanh(n * (GELU_A + (GELU_A * GELU_B) * square))
    half = 0.5 + 0.5 * t
    act = n * half
    slope = half + (0.5 * n) * (1.0 - t * t) * (GELU_A + (3.0 * GELU_A * GELU_B) * square)
    return act, slope, xhat, rstd


def rows_back(u, slope, xhat, rstd):
    t = slope * u
    m1 = jnp.sum(t, axis=-1, keepdims=True) * (1.0 / D)
    m2 = jnp.sum(t * xhat, axis=-1, keepdims=True) * (1.0 / D)
    return rstd * (t - m1 - xhat * m2)


def step_kernel(
    blocks_ref, ids_ref, live_ref, positives_ref, patches_ref, w_hbm, bias_ref, gain_ref, ibias_hbm,
    users_hbm, proj_hbm,
    duser_ref, out_ref, bout_ref, gout_ref,
    main, tails, send, recv, tsend, trecv, trows, xtail, psend, precv, dsend, drecv,
    proj, xhat_m, slope_m, rstd_m, act_t, xhat_t, slope_t, rstd_t, dtail, gsum, dlow, dlow_t, uvec, dbacc, g,
    w_ref, ibias_ref, users_ref, proj_ref, proj_t, uvec_t, belongs_t, xt, xt_t,
    sx, rx, relay, sy, ry, accx, sz, rz, vown, vx, vy, vz,
    sem_s, sem_r, sem_ts, sem_tr, sem_ps, sem_pr, sem_ds, sem_dr,
    sem_sx, sem_rx, sem_sy, sem_ry, sem_z, sem_vsx, sem_vrx, sem_vsy, sem_vry, sem_vz, sem_load,
):
    dp = lax.axis_index("dp")
    enc = lax.axis_index("enc")
    x = dp // (NY * NZ)
    y = (dp // NZ) % NY
    z = dp % NZ
    core = enc % 2
    ring = z * 6 + enc // 2

    def at(xx, yy, zz):
        return {"dp": (xx * NY + yy) * NZ + zz}

    def on_ring(place, which):
        place = (place + 12) % 12
        return {"dp": (x * NY + y) * NZ + place // 6, "enc": (place % 6) * 2 + which}

    def dest(p, r):
        return on_ring(ring + offset(p, core), (core + r) % 2)

    def source(p, r):
        other = (core + r) % 2
        return on_ring(ring - offset(p, other), other)

    loads = [
        pltpu.make_async_copy(there, here, sem_load.at[n])
        for n, (there, here) in enumerate(
            [(users_hbm, users_ref), (proj_hbm, proj_ref), (ibias_hbm, ibias_ref), (w_hbm, w_ref)])
    ]
    barrier = pltpu.get_barrier_semaphore()
    partners = 0
    for p in range(6):
        for r in range(2):
            if p or r:
                pl.semaphore_signal(barrier, inc=1, device_id=source(p, r))
                partners += 1
    for d in range(1, NX):
        pl.semaphore_signal(barrier, inc=1, device_id=at((x + d) % NX, y, z))
    for d in range(1, NY):
        pl.semaphore_signal(barrier, inc=1, device_id=at(x, (y + d) % NY, z))
    pl.semaphore_signal(barrier, inc=1, device_id=at(x, y, 1 - z))
    partners += NX + NY - 1
    for load in loads:
        load.start()

    n_live = live_ref[0] * BLOCKS_ITEM
    named = [jnp.where(b < n_live, blocks_ref[b], -1) for b in range(BLOCKS_DEV)]
    src = []
    lane_slot = lax.broadcasted_iota(jnp.int32, (1, N_ENC * 16), 1) >> 3
    items = jnp.full((1, N_ENC * 16), -1, jnp.int32)
    for j in range(N_ENC):
        expert = dest(j // 2, j % 2)["enc"]
        low, high = jnp.int32(BLOCKS_DEV), jnp.int32(-1)
        for b in range(BLOCKS_DEV):
            high = jnp.where(named[b] == expert, b, high)
            back = BLOCKS_DEV - 1 - b
            low = jnp.where(named[back] == expert, back, low)
        src.append(jnp.minimum(low, BLOCKS_DEV - 1))
        src.append(jnp.maximum(high, 0))
        items = jnp.where(lane_slot == 2 * j, jnp.where(low < BLOCKS_DEV, low >> 2, -1), items)
        items = jnp.where(lane_slot == 2 * j + 1, jnp.where(high > low, high >> 2, -1), items)

    tails[...] = jnp.zeros_like(tails)
    row = lax.broadcasted_iota(jnp.int32, (208, PATCHES), 0)
    col = lax.broadcasted_iota(jnp.int32, (208, PATCHES), 1)
    steps = (row >= 48).astype(jnp.int32) + (row >= 96).astype(jnp.int32) + (row >= 144).astype(jnp.int32)
    origin = jnp.where(row < 192, row + steps, (row - 192) * BLOCK_ROWS + MAIN)
    order = jnp.where(origin == col, 1.0, 0.0).astype(bf16)
    for i in range(ITEMS_DEV):
        sorted_rows = jnp.dot(order, patches_ref[:, i, :], preferred_element_type=f32)
        for b in range(BLOCKS_ITEM):
            main[i * BLOCKS_ITEM + b] = sorted_rows[b * MAIN : (b + 1) * MAIN].astype(bf16)
            tails[i * BLOCKS_ITEM + b] = row_to_tile(sorted_rows[192 + b : 193 + b])

    def remote(src, dst, ssem, rsem, device):
        return pltpu.make_async_remote_copy(
            src_ref=src, dst_ref=dst, send_sem=ssem, recv_sem=rsem, device_id=device)

    def tail_tile(j):
        return jnp.concatenate([tails[src[2 * j]], tails[src[2 * j + 1]]], axis=0).astype(bf16)

    trecv[0] = tail_tile(0)
    for j in range(1, N_ENC):
        tsend[j] = tail_tile(j)
    pl.semaphore_wait(barrier, partners)
    started = []

    def start(copy):
        copy.start()
        started.append(copy)
        return copy

    for p in (5, 4, 3, 2, 1, 0):
        if p == 5:
            for j in range(1, N_ENC):
                start(remote(tsend.at[j], trecv.at[j], sem_ts.at[j], sem_tr.at[j], dest(j // 2, j % 2)))
        for r in range(2):
            j = 2 * p + r
            if j:
                for k in range(CAP):
                    send[j, k] = main[src[2 * j + k]]
                start(remote(send.at[j], recv.at[j], sem_s.at[j], sem_r.at[j], dest(p, r)))
    for k in range(CAP):
        recv[0, k] = main[src[k]]

    for load in loads:
        load.wait()

    @pl.loop(0, D // 256)
    def _(m):
        first = pl.multiple_of(m * 256, 256)
        uvec[:, pl.ds(first, 256)] = jnp.dot(
            users_ref[...], proj_ref[:, pl.ds(first, 256)], preferred_element_type=f32).astype(bf16)

    @pl.loop(0, PIECES)
    def _(c):
        lanes = pl.ds(pl.multiple_of(c * LANES, LANES), LANES)
        proj_t[lanes, :] = proj_ref[:, lanes].T

    entry = lax.broadcasted_iota(jnp.int32, (512, LANES), 0) * LANES + lax.broadcasted_iota(jnp.int32, (512, LANES), 1)
    item_row = lax.broadcasted_iota(jnp.int32, (8, 1), 0)
    item_biases = jnp.zeros((8, 1), f32)
    for i in range(ITEMS_DEV):
        picked = jnp.where(entry == ids_ref[i], ibias_ref[...], 0.0)
        picked = jnp.sum(jnp.sum(picked, axis=0, keepdims=True), axis=1, keepdims=True)
        item_biases = item_biases + jnp.where(item_row == i, picked, 0.0)

    out_row = lax.broadcasted_iota(jnp.int32, (48, N_ENC * 16), 0)
    in_col = lax.broadcasted_iota(jnp.int32, (48, N_ENC * 16), 1)
    belongs = ((out_row & 7) == items) & ((out_row >> 3) == (in_col & 7))
    belongs = jnp.where(belongs, 1.0, 0.0).astype(bf16)

    belongs_t[...] = belongs.astype(f32).T.astype(bf16)
    for c in range(PIECES):
        uvec_t[c * LANES : (c + 1) * LANES, :] = uvec[:, c * LANES : (c + 1) * LANES].T

    bias = bias_ref[...]
    gain = gain_ref[...]

    trows[...] = jnp.zeros_like(trows)
    for j in range(N_ENC):
        if j:
            remote(tsend.at[j], trecv.at[j], sem_ts.at[j], sem_tr.at[j], dest(j // 2, j % 2)).wait_recv()
        tile = trecv[j].astype(f32)
        for k in range(CAP):
            trows[2 * j + k : 2 * j + k + 1, :] = tile_to_row(tile[8 * k : 8 * k + 8])
    xtail[...] = trows[...].astype(bf16)
    xt_t[...] = trows[...].T.astype(bf16)
    proj[0:32, :] = jnp.dot(xtail[...], w_ref[...], preferred_element_type=f32)
    for s in range(2):
        rows = slice(s * GROUP, (s + 1) * GROUP)
        act, slope, xhat, rstd = normed_rows(proj[rows, :], bias, gain)
        act_t[rows, :] = act
        slope_t[rows, :] = slope
        xhat_t[rows, :] = xhat
        rstd_t[rows, :] = jnp.broadcast_to(rstd, (GROUP, LANES))

    def forward(q, carry):
        p = (6 - q) % 6
        for r in range(2):
            @pl.when(2 * p + r > 0)
            def _():
                remote(send.at[2 * p + r], recv.at[2 * p + r], sem_s.at[2 * p + r], sem_r.at[2 * p + r],
                       {"enc": (enc // 2) * 2 + 1 - core}).wait_recv()
        @pl.loop(0, D // 256, unroll=True)
        def _(m):
            first = pl.multiple_of(m * 256, 256)
            proj[:, pl.ds(first, 256)] = jnp.dot(
                recv[pl.ds(2 * p, 2)].reshape(4 * MAIN, D), w_ref[:, pl.ds(first, 256)], preferred_element_type=f32)

        def slot(s, carry):
            own = 4 * p + s
            pooled = act_t[pl.ds(own, 1), :]
            weighted = slope_t[pl.ds(own, 1), :] * xhat_t[pl.ds(own, 1), :]
            pool, gs = None, None
            for m in range(MAIN // GROUP):
                act, slope, xhat, rstd = normed_rows(
                    proj[pl.ds(pl.multiple_of(s * MAIN + m * GROUP, GROUP), GROUP), :], bias, gain)
                rows = slice(m * GROUP, (m + 1) * GROUP)
                slope_m[own, rows, :] = slope
                xhat_m[own, rows, :] = xhat
                rstd_m[own, rows, :] = jnp.broadcast_to(rstd, (GROUP, LANES))
                product = slope * xhat
                act = act[0:8] + act[8:16]
                product = product[0:8] + product[8:16]
                pool = act if pool is None else pool + act
                gs = product if gs is None else gs + product
            gsum[pl.ds(own, 1), :] = jnp.sum(gs, axis=0, keepdims=True) + weighted
            trows[pl.ds(own, 1), :] = jnp.sum(pool, axis=0, keepdims=True) + pooled
            return carry
        lax.fori_loop(0, 4, slot, 0, unroll=True)
        for r in range(2):
            j = 2 * p + r
            tile = jnp.concatenate(
                [row_to_tile(trows[pl.ds(2 * j + k, 1), :]) for k in range(CAP)], axis=0).astype(bf16)
            psend[j] = tile
            if r == 0:
                @pl.when(p == 0)
                def _():
                    precv[0] = tile

            @pl.when(j > 0)
            def _():
                remote(psend.at[j], precv.at[j], sem_ps.at[j], sem_pr.at[j], source(p, r)).start()
        return carry
    lax.fori_loop(0, 6, forward, 0)

    returned = [remote(psend.at[j], precv.at[j], sem_ps.at[j], sem_pr.at[j], source(j // 2, j % 2)) for j in range(1, N_ENC)]

    def turn(c, carry):
        lanes = pl.ds(pl.multiple_of(c * LANES, LANES), LANES)
        xt[lanes, :] = recv[:, :, :, lanes].reshape(SLOTS * MAIN, LANES).T
        return carry
    lax.fori_loop(0, PIECES // 2, turn, 0)
    for copy in returned:
        copy.wait_recv()
    summed = jnp.dot(belongs, precv[...].reshape(N_ENC * 16, LANES), preferred_element_type=f32)
    embed = jnp.concatenate([summed[8 * c : 8 * c + 8] for c in range(PIECES)], axis=1)
    embed = (embed / PATCHES).astype(bf16)
    scores = jnp.dot(embed, uvec_t[...], preferred_element_type=f32)
    scores = scores * score_scale + item_biases
    index = lax.broadcasted_iota(jnp.int32, (8, USERS_DEV), 0)
    chosen = positives_ref[...].astype(f32)
    chosen = jnp.concatenate([chosen[0:1], chosen[1:2]], axis=1)
    live = live_ref[0].astype(f32)
    chosen = chosen - live * jnp.floor((chosen + 0.5) / live)
    target = jnp.where(index.astype(f32) == chosen, 1.0, 0.0)
    sigmoid = 1.0 / (1.0 + jnp.exp(-scores))
    d_score = jnp.where(index < live_ref[0], loss_weight * (sigmoid - target), 0.0).astype(bf16)
    d_embed = jnp.dot(d_score, uvec[...], preferred_element_type=f32) * score_scale
    d_folded = jnp.concatenate([d_embed[:, c * LANES : (c + 1) * LANES] for c in range(PIECES)], axis=0).astype(bf16)
    d_slots = jnp.dot(belongs_t[...], d_folded, preferred_element_type=f32)
    dsend[...] = d_slots.astype(bf16).reshape(N_ENC, 16, LANES)
    for p in (5, 4, 3, 2, 1, 0):
        for r in range(2):
            j = 2 * p + r
            if j:
                start(remote(dsend.at[j], drecv.at[j], sem_ds.at[j], sem_dr.at[j], dest(p, r)))
    drecv[0] = dsend[0]
    lax.fori_loop(PIECES // 2, PIECES, turn, 0)

    dtail[...] = jnp.zeros_like(dtail)
    dbacc[...] = jnp.zeros_like(dbacc)

    def backward(j, done):
        carry = None
        @pl.when(j > 0)
        def _():
            remote(dsend.at[j], drecv.at[j], sem_ds.at[j], sem_dr.at[j],
                   {"enc": (enc // 2) * 2 + 1 - core}).wait_recv()
        tile = drecv[j].astype(f32) / PATCHES
        for k in range(CAP):
            own = 2 * j + k
            d_row = tile_to_row(tile[8 * k : 8 * k + 8])
            dtail[pl.ds(own, 1), :] = d_row
            u = d_row * gain
            for m in range(MAIN // GROUP):
                rows = slice(m * GROUP, (m + 1) * GROUP)
                rstd = jnp.concatenate([rstd_m[own, rows, :]] * PIECES, axis=1)
                d_projected = rows_back(u, slope_m[own, rows, :], xhat_m[own, rows, :], rstd)
                dlow[own, rows, :] = d_projected.astype(bf16)
                part = d_projected[0:8] + d_projected[8:16]
                carry = part if carry is None else carry + part
        dbacc[...] += carry
        return done
    lax.fori_loop(0, N_ENC, backward, 0, unroll=2)
    for s in range(2):
        rows = slice(s * GROUP, (s + 1) * GROUP)
        rstd = jnp.concatenate([rstd_t[rows, :]] * PIECES, axis=1)
        d_projected = rows_back(dtail[rows, :] * gain, slope_t[rows, :], xhat_t[rows, :], rstd)
        dlow_t[rows, :] = d_projected.astype(bf16)
        dbacc[...] += d_projected[0:8] + d_projected[8:16]
    d_bias = jnp.sum(dbacc[...], axis=0, keepdims=True)
    d_gain = jnp.sum(dtail[0:SLOTS, :] * gsum[0:SLOTS, :], axis=0, keepdims=True)
    vectors = jnp.concatenate([row_to_tile(d_bias), row_to_tile(d_gain)], axis=0)

    vown[...] = vectors
    vx[x] = vectors
    vectors_x = [remote(vown, vx.at[x], sem_vsx.at[d - 1], sem_vrx.at[d - 1], at((x + d) % NX, y, z)) for d in range(1, NX)]
    for copy in vectors_x:
        copy.start()

    def pack(h, xx):
        @pl.loop(0, NY, unroll=True)
        def _(k):
            first = pl.multiple_of((xx * NY + k) * 24, 8)
            chunk = g[pl.ds(first, 24), :]
            sx[h, xx, k] = jnp.concatenate([fold(chunk[0:12]), fold(chunk[12:24])], axis=0).astype(bf16)

    left, right, far = (x + 3) % NX, (x + 1) % NX, (x + 2) % NX
    low, high = pl.ds(0, NY // 2), pl.ds(NY // 2, NY // 2)

    def along_x(h, n):
        source_ref, to = [
            (sx.at[h, far, low], left), (sx.at[h, far, high], right),
            (sx.at[h, right, low], right), (sx.at[h, left, high], left),
            (relay.at[h, 0], left), (relay.at[h, 1], right),
        ][n]
        return remote(source_ref, rx.at[h, n], sem_sx.at[h, n], sem_rx.at[h, n], at(to, y, z))

    def pass_on(h):
        for n in range(2):
            along_x(h, n).wait_recv()
            half = sx[h, left, low] if n == 0 else sx[h, right, high]
            relay[h, n] = (rx[h, n].astype(f32) + half.astype(f32)).astype(bf16)
            along_x(h, 4 + n).start()

    def along_y(h, d):
        to = (y + d) % NY
        return remote(sy.at[h, to], ry.at[h, d - 1], sem_sy.at[h, d - 1], sem_ry.at[h, d - 1], at(x, to, z))

    def along_z(h):
        return remote(sz.at[h, 1 - z], rz.at[h], sem_z.at[h, 0], sem_z.at[h, 1], at(x, y, 1 - z))

    vectors_y = [remote(vy.at[y], vy.at[y], sem_vsy.at[d - 1], sem_vry.at[d - 1], at(x, (y + d) % NY, z)) for d in range(1, NY)]
    vectors_z = remote(vz.at[0], vz.at[1], sem_vz.at[0], sem_vz.at[1], at(x, y, 1 - z))

    def piece(h, carry):
        lanes = pl.ds(pl.multiple_of(h * PIECE, PIECE), PIECE)
        g[...] = jnp.dot(
            xt[...], dlow[:, :, lanes].reshape(SLOTS * MAIN, PIECE), preferred_element_type=f32) + jnp.dot(
            xt_t[...], dlow_t[:, lanes], preferred_element_type=f32)
        pack(h, far)
        along_x(h, 0).start()
        along_x(h, 1).start()
        pack(h, right)
        along_x(h, 2).start()
        pack(h, left)
        along_x(h, 3).start()
        pack(h, x)

        @pl.when(h > 0)
        def _():
            pass_on(h - 1)
        return carry
    lax.fori_loop(0, N_PIECES, piece, 0)

    def sum_x(h):
        for n in range(2, 6):
            along_x(h, n).wait_recv()

        @pl.loop(0, NY // 2, unroll=True)
        def _(k):
            for n in range(2):
                own = k + n * (NY // 2)
                total = sx[h, x, own].astype(f32) + (rx[h, 2 + n, k].astype(f32) + rx[h, 4 + n, k].astype(f32))
                accx[h, own] = total
                sy[h, own] = total.astype(bf16)
        for d in (4, 3, 5, 2, 6, 1, 7):
            along_y(h, d).start()

    def sum_y(h):
        total = accx[h, y]
        for d in range(1, NY):
            along_y(h, d).wait_recv()
            total = total + ry[h, d - 1].astype(f32)
        sz[h, 0] = total[0:8]
        sz[h, 1] = total[8:16]
        along_z(h).start()

    for copy in vectors_x:
        copy.wait_recv()
    vy[y] = (vx[0] + vx[1]) + (vx[2] + vx[3])
    for copy in vectors_y:
        copy.start()
    sum_x(0)
    pass_on(N_PIECES - 1)
    sum_x(1)
    sum_x(2)
    for copy in vectors_y:
        copy.wait_recv()
    vz[0] = ((vy[0] + vy[1]) + (vy[2] + vy[3])) + ((vy[4] + vy[5]) + (vy[6] + vy[7]))
    vectors_z.start()
    d_user_vec = lax.dot_general(d_score, embed, (((0,), (0,)), ((), ())), preferred_element_type=f32)
    uvec[...] = (d_user_vec * score_scale).astype(bf16)

    @pl.loop(0, D // 256)
    def _(m):
        lanes = pl.ds(pl.multiple_of(m * 256, 256), 256)
        duser_ref[:, lanes] = jnp.dot(uvec[...], proj_t[:, lanes], preferred_element_type=f32).astype(bf16)

    for h in range(N_PIECES):
        sum_y(h)
    scale = 1.0 / (NX * NY * NZ)
    vectors_z.wait_recv()
    folded = (vz[0] + vz[1]) * scale
    bout_ref[...] = tile_to_row(folded[0:8])
    gout_ref[...] = tile_to_row(folded[8:16])
    for h in range(N_PIECES):
        along_z(h).wait_recv()
        rows = unfold((sz[h, z] + rz[h]) * scale)
        for r in range(ROWS_DEV):
            out_ref[r, :, h * PIECE : (h + 1) * PIECE] = rows[r : r + 1]
    for copy in started + returned + vectors_x + vectors_y + [vectors_z]:
        copy.wait_send()
    for h in range(N_PIECES):
        for n in range(6):
            along_x(h, n).wait_send()
        for d in range(1, NY):
            along_y(h, d).wait_send()
        along_z(h).wait_send()


def copy_kernel(*refs):
    n = len(refs) // 2
    copies = [pltpu.make_async_copy(refs[i], refs[n + i], refs[-1].at[i]) for i in range(n)]
    for copy in copies:
        copy.start()
    for copy in copies:
        copy.wait()


def copy_out(arrays):
    return pl.pallas_call(
        copy_kernel,
        out_shape=[jax.ShapeDtypeStruct(a.shape, a.dtype) for a in arrays],
        in_specs=[pl.BlockSpec(memory_space=pltpu.VMEM)] * len(arrays),
        out_specs=[pl.BlockSpec(memory_space=pl.ANY)] * len(arrays),
        scratch_shapes=[pltpu.SemaphoreType.DMA((len(arrays),))],
        compiler_params=pltpu.CompilerParams(vmem_limit_bytes=2 * 1024 * 1024),
        name="copy_out",
    )(*arrays)


def train_step(blocks, ids, live, positives, patches, weight, bias, gain, item_bias, users, proj):
    vmem = pl.BlockSpec(memory_space=pltpu.VMEM)
    smem = pl.BlockSpec(memory_space=pltpu.SMEM)
    anywhere = pl.BlockSpec(memory_space=pl.ANY)
    dma = pltpu.SemaphoreType.DMA
    return pl.pallas_call(
        step_kernel,
        out_shape=(
            pltpu.VMEM((USERS_DEV, D), bf16),
            pltpu.VMEM((ROWS_DEV, 1, D), f32),
            pltpu.VMEM((1, D), f32),
            pltpu.VMEM((1, D), f32),
        ),
        in_specs=[smem] * 3 + [vmem] * 2 + [anywhere] + [vmem] * 2 + [anywhere] * 3,
        out_specs=[vmem] * 4,
        scratch_shapes=[
            pltpu.VMEM((BLOCKS_DEV, MAIN, D), bf16),
            pltpu.VMEM((BLOCKS_DEV, 8, LANES), f32),
            pltpu.VMEM((N_ENC, CAP, MAIN, D), bf16),
            pltpu.VMEM((N_ENC, CAP, MAIN, D), bf16),
        ] + [pltpu.VMEM((N_ENC, 16, LANES), bf16)] * 2 + [
            pltpu.VMEM((32, D), f32),
            pltpu.VMEM((32, D), bf16),
        ] + [pltpu.VMEM((N_ENC, 16, LANES), bf16)] * 4 + [
            pltpu.VMEM((4 * MAIN, D), f32),
            pltpu.VMEM((SLOTS, MAIN, D), f32),
            pltpu.VMEM((SLOTS, MAIN, D), f32),
            pltpu.VMEM((SLOTS, MAIN, LANES), f32),
            pltpu.VMEM((32, D), f32),
            pltpu.VMEM((32, D), f32),
            pltpu.VMEM((32, D), f32),
            pltpu.VMEM((32, LANES), f32),
            pltpu.VMEM((32, D), f32),
            pltpu.VMEM((32, D), f32),
            pltpu.VMEM((SLOTS, MAIN, D), bf16),
            pltpu.VMEM((32, D), bf16),
            pltpu.VMEM((USERS_DEV, D), bf16),
            pltpu.VMEM((8, D), f32),
            pltpu.VMEM((D, PIECE), f32),
            pltpu.VMEM((D, D), bf16),
            pltpu.VMEM((512, LANES), f32),
            pltpu.VMEM((USERS_DEV, D), bf16),
            pltpu.VMEM((D, D), bf16),
            pltpu.VMEM((D, D), bf16),
            pltpu.VMEM((D, USERS_DEV), bf16),
            pltpu.VMEM((N_ENC * 16, 48), bf16),
            pltpu.VMEM((D, SLOTS * MAIN), bf16),
            pltpu.VMEM((D, 32), bf16),
            pltpu.VMEM((N_PIECES, NX, NY, 16, FOLD), bf16),
            pltpu.VMEM((N_PIECES, 6, NY // 2, 16, FOLD), bf16),
            pltpu.VMEM((N_PIECES, 2, NY // 2, 16, FOLD), bf16),
            pltpu.VMEM((N_PIECES, NY, 16, FOLD), bf16),
            pltpu.VMEM((N_PIECES, NY - 1, 16, FOLD), bf16),
            pltpu.VMEM((N_PIECES, NY, 16, FOLD), f32),
            pltpu.VMEM((N_PIECES, 2, 8, FOLD), f32),
            pltpu.VMEM((N_PIECES, 8, FOLD), f32),
            pltpu.VMEM((16, LANES), f32),
            pltpu.VMEM((NX, 16, LANES), f32),
            pltpu.VMEM((NY, 16, LANES), f32),
            pltpu.VMEM((2, 16, LANES), f32),
        ] + [dma((N_ENC,))] * 8 + [
            dma((N_PIECES, 6)), dma((N_PIECES, 6)), dma((N_PIECES, NY - 1)), dma((N_PIECES, NY - 1)),
            dma((N_PIECES, 2)),
            dma((NX - 1,)), dma((NX - 1,)), dma((NY - 1,)), dma((NY - 1,)), dma((2,)), dma((4,)),
        ],
        compiler_params=pltpu.CompilerParams(
            collective_id=0, has_side_effects=True, vmem_limit_bytes=56 * 1024 * 1024),
        name="train_step",
    )(blocks, ids, live, positives, patches, weight, bias, gain, item_bias, users, proj)


def body(
    patches,
    item_counts,
    item_ids,
    block_dest,
    enc_weight,
    enc_bias,
    enc_gain,
    item_bias,
    user_state,
    user_proj,
    positives,
):
    outs = train_step(
        block_dest, item_ids, item_counts, positives.reshape(-1, LANES), jnp.transpose(patches, (1, 0, 2)), enc_weight[0], enc_bias, enc_gain,
        item_bias.reshape(-1, LANES), user_state, user_proj)
    d_user, mine, d_bias, d_gain = copy_out(outs)
    return (d_user, jnp.transpose(mine, (1, 0, 2)), d_bias, d_gain)


def solution(mesh):
    return jax.shard_map(
        body,
        mesh=mesh,
        in_specs=(
            P(("dp", "enc"), None, None),
            P(("dp", "enc")),
            P(("dp", "enc")),
            P(("dp", "enc")),
            P("enc", None, None),
            P("enc", None),
            P("enc", None),
            P(),
            P(("dp", "enc"), None),
            P(),
            P(("dp", "enc")),
        ),
        out_specs=(P(("dp", "enc"), None), P("enc", "dp", None), P("enc", None), P("enc", None)),
        check_vma=False,
    )
```
